512 devices in a mesh: grp: 16 (over x_lo, y), seq: 32 (over x_hi, z, core).
Axes of the slice: x: 4 (x_hi: 2, x_lo: 2; x = x_hi * 2 + x_lo), y: 8, z: 8, core: 2. Of those that a mesh axis runs over, the one named last changes fastest.
Arguments:
- tokens: bfloat16 [16, 12288, 1536], P('grp', 'seq'), may hold values from -32 to 32, as said below
- router: bfloat16 [1536, 512], P('grp'), may hold values from -1 to 1, as said below
- norm_gain: float32 [32, 1536], P('seq'), may hold values from 0.1 to 1.9
- w_in: bfloat16 [32, 1536, 6144], P('seq', None, 'grp'), may hold values from -0.15625 to 0.15625
- w_out: bfloat16 [32, 6144, 1536], P('seq', 'grp'), may hold values from -0.078125 to 0.078125
Outputs:
- output: bfloat16 [16, 12288, 1536], P('grp', 'seq')
The draws below stay inside these ranges and needn't reach their ends.
Inputs may be any that keep to these rules, and one draw needn't show every extreme that they name: `tokens`: token features are real values. `router`: slot parameters are real values.
All inputs are finite; a program needn't handle non-finite values.
Results may differ from the reference program's by a relative error of at most 0.0075.
Values may be sent and summed in bfloat16 or wider, within the bound.
No kernel may reach another device: no remote copies, remote signals or barrier semaphores. Data moves between devices by JAX's collectives and lax.ppermute only.
A program may use at most 64 MiB of HBM per device.

```python
import math
import jax
import jax.numpy as jnp
from jax import lax

D = 1536
FF = 6144
SLOT_EXP = 16
EXPERTS = 32
SLOTS = 512
GROUPS = 16
TOKENS = 12288
FF_DEV = 384
N_GRP = 16


def joint_draw(key):
    base = jax.random.fold_in(key, 4711)
    keys = jax.random.split(base, 2)
    feats = jax.random.normal(keys[0], (GROUPS, TOKENS, D), jnp.float32)
    mixer = jnp.clip(jax.random.normal(keys[1], (D, SLOTS), jnp.float32), -4.0, 4.0) * (2.5 / math.sqrt(D))
    limit = 1.0 + 400 // D
    feats = jnp.clip(feats, -6.0, 6.0)
    mixer = jnp.clip(mixer, -limit, limit)
    return (feats, mixer)


def draw_tokens(key, part):
    return joint_draw(key)[0].astype(jnp.bfloat16)


def draw_router(key, part):
    return joint_draw(key)[1].astype(jnp.bfloat16)


def block_levels(own_key, dims, pieces, low, top_value):
    def one(axis_at, shards_of):
        steps = jax.random.uniform(jax.random.fold_in(jax.random.fold_in(own_key, 6), axis_at), (shards_of,), jnp.float32, low / len(pieces), top_value / len(pieces))
        return jnp.repeat(jnp.exp(steps), dims[axis_at] // shards_of).reshape((-1,) + (1,) * (len(dims) - axis_at - 1))

    factor_of = one(*pieces[0])
    for cut in pieces[1:]:
        factor_of = factor_of * one(*cut)
    return factor_of


def gaussian(stream_key, extent, width, most, pieces=(), dtype=jnp.bfloat16):
    factor_of = block_levels(stream_key, extent, pieces, -0.22, 0.18) if pieces else 1.0
    entries = jax.random.normal(stream_key, extent, jnp.float32) * width * factor_of
    return jnp.minimum(jnp.maximum(entries, -most), most).astype(dtype)


def setup_inputs(seed: int = 0) -> dict:
    splits = jax.random.split(jax.random.key(seed), 6)
    tokens = draw_tokens(jax.random.fold_in(splits[5], 71), 0)
    router = draw_router(jax.random.fold_in(splits[5], 71), 0)
    norm_gain = jnp.clip(1.0 + 0.18 * jax.random.normal(splits[2], (EXPERTS, D), jnp.float32), 0.1, 1.9)
    w_in = gaussian(splits[3], (EXPERTS, D, FF), D ** -0.5, 0.15625, ((0, 32), (2, 16)))
    w_out = gaussian(splits[4], (EXPERTS, FF, D), FF ** -0.5, 0.078125, ((0, 32), (1, 16)))
    return {"tokens": tokens, "router": router, "norm_gain": norm_gain, "w_in": w_in, "w_out": w_out}


def reference(tokens, router, norm_gain, w_in, w_out):

    def dispatch_group(feats):
        logits = jnp.dot(feats, router, preferred_element_type=jnp.float32)
        highest = lax.optimization_barrier(jnp.max(logits, axis=0, keepdims=True))
        dispatch = jnp.exp(logits - highest).astype(jnp.bfloat16)
        return jnp.dot(dispatch.T, feats, preferred_element_type=jnp.float32)
    pooled = lax.map(dispatch_group, tokens)
    pooled = pooled.reshape(GROUPS, EXPERTS, SLOT_EXP, D)
    mean_sq = lax.optimization_barrier(jnp.mean(pooled * pooled, axis=-1, keepdims=True))
    slots = (pooled * lax.rsqrt(mean_sq + 1e-06) * norm_gain[None, :, None, :]).astype(jnp.bfloat16)

    def run_expert(operands):
        expert_slots, weight_in, weight_out = operands
        gathered = expert_slots.reshape(GROUPS * SLOT_EXP, D)
        hidden = jax.nn.gelu(jnp.dot(gathered, weight_in, preferred_element_type=jnp.float32)).astype(jnp.bfloat16)
        blocks = hidden.reshape(GROUPS * SLOT_EXP, N_GRP, FF_DEV).transpose(1, 0, 2).astype(jnp.float32)
        out_blocks = weight_out.reshape(N_GRP, FF_DEV, D).astype(jnp.float32)
        parts = jnp.einsum('krf,kfd->krd', blocks, out_blocks, precision=lax.Precision.HIGHEST)
        rounded = lax.optimization_barrier(parts.astype(jnp.bfloat16)).astype(jnp.float32)
        return lax.optimization_barrier(jnp.sum(rounded, axis=0)).astype(jnp.bfloat16).reshape(GROUPS, SLOT_EXP, D)
    expert_out = lax.map(run_expert, (slots.transpose(1, 0, 2, 3), w_in, w_out))
    expert_out = expert_out.transpose(1, 0, 2, 3).reshape(GROUPS, SLOTS, D)

    def combine_group(operands):
        feats, outputs = operands
        logits = jnp.dot(feats, router, preferred_element_type=jnp.float32)
        weights = jax.nn.softmax(logits, axis=1).astype(jnp.bfloat16)
        mixed = jnp.dot(weights, outputs, preferred_element_type=jnp.float32)
        return (feats.astype(jnp.float32) + mixed).astype(jnp.bfloat16)
    return lax.map(combine_group, (tokens, expert_out))
```

```python
import jax
import jax.numpy as jnp
from jax import lax
from jax.sharding import Mesh, PartitionSpec as P

F32 = jnp.float32
BF16 = jnp.bfloat16
EXTRA = 128


def other(length=2):
    return [(k, k ^ 1) for k in range(length)]


def pieces(value):
    first = lax.reduce_precision(value, 8, 7)
    second = lax.reduce_precision(value - first, 8, 7)
    third = value - first - second
    return first, second, third


def with_pieces(body, columns):
    parts = [p[..., None] for column in columns for p in pieces(column)]
    fill = jnp.zeros((*body.shape[:-1], EXTRA - len(parts)), F32)
    return jnp.concatenate([body, *parts, fill], axis=-1).astype(BF16)


def piece_sum(block, which):
    part = block[..., 3 * which : 3 * which + 3].astype(F32)
    return part[..., 0] + part[..., 1] + part[..., 2]


def sent_to_all(value, axes):
    length = lax.axis_size(axes)
    return lax.all_to_all(
        jnp.broadcast_to(value[None], (length, *value.shape)), axes, 0, 0, tiled=True
    )


def local(tokens, router, norm_gain, w_in, w_out):
    feats = tokens[0]
    count, width = feats.shape
    slot_count = router.shape[1]
    owners = lax.axis_size(("xhi", "z"))
    per_owner = slot_count // (2 * owners)
    half = slot_count // 2
    core = lax.axis_index("core")

    partner_feats = lax.ppermute(feats, "core", other())
    partner_in = lax.ppermute(w_in[0], "xlo", other())
    partner_out = lax.ppermute(w_out[0], "xlo", other())

    row = lax.broadcasted_iota(jnp.int32, (slot_count, half), 0)
    col = lax.broadcasted_iota(jnp.int32, (slot_count, half), 1)
    wanted = (col // per_owner * 2 + core) * per_owner + col % per_owner
    pick = (row == wanted).astype(BF16)
    own_columns = jnp.dot(router, pick, preferred_element_type=F32).astype(BF16)
    columns = sent_to_all(own_columns, ("xlo", "y")).reshape(width, half)

    logits = jnp.dot(feats, columns, preferred_element_type=F32)
    partner_logits = jnp.dot(partner_feats, columns, preferred_element_type=F32)
    high = jnp.maximum(jnp.max(logits, axis=0), jnp.max(partner_logits, axis=0))
    dispatch = jnp.exp(logits - high).astype(BF16)
    partner_dispatch = jnp.exp(partner_logits - high).astype(BF16)
    dims = (((0,), (0,)), ((), ()))
    sums = lax.dot_general(dispatch, feats, dims, preferred_element_type=F32)
    sums += lax.dot_general(partner_dispatch, partner_feats, dims, preferred_element_type=F32)
    message = with_pieces(sums, [high]).reshape(owners, per_owner, width + EXTRA)
    received = lax.all_to_all(message, ("xhi", "z"), 0, 0, tiled=True)

    row_high = jnp.max(logits, axis=1)
    exps = jnp.exp(logits - row_high[:, None])
    row_sum = jnp.sum(exps, axis=1)
    partner_high = jnp.max(partner_logits, axis=1)
    partner_exps = jnp.exp(partner_logits - partner_high[:, None])
    answer = with_pieces(partner_exps, [partner_high, jnp.sum(partner_exps, axis=1)])
    answer = lax.ppermute(answer, "core", other())

    highs = piece_sum(received[:, :, width:], 0)
    overall = jnp.max(highs, axis=0)
    scale = jnp.exp(highs - overall)
    pooled = jnp.sum(received[:, :, :width].astype(F32) * scale[:, :, None], axis=0)
    mean_sq = jnp.mean(pooled * pooled, axis=-1, keepdims=True)
    slots = (pooled * lax.rsqrt(mean_sq + 1e-06) * norm_gain[0]).astype(BF16)

    rows = sent_to_all(slots, "y")
    groups = rows.shape[0]
    rows = rows.reshape(groups * per_owner, width)
    hidden = jax.nn.gelu(jnp.dot(rows, w_in[0], preferred_element_type=F32)).astype(BF16)
    hidden_b = jax.nn.gelu(jnp.dot(rows, partner_in, preferred_element_type=F32)).astype(BF16)
    partial = jnp.dot(hidden, w_out[0], preferred_element_type=F32)
    partial += jnp.dot(hidden_b, partner_out, preferred_element_type=F32)
    partial = partial.astype(BF16).reshape(groups, per_owner, width)
    blocks = lax.all_to_all(partial, "y", 0, 0, tiled=True)
    own_out = jnp.sum(blocks.astype(F32), axis=0).astype(BF16)

    outs = sent_to_all(own_out, ("xhi", "z")).reshape(half, width)
    outs_b = lax.ppermute(outs, "core", other())

    exps_b = answer[:, :half]
    row_high_b = piece_sum(answer[:, half:], 0)
    row_sum_b = piece_sum(answer[:, half:], 1)
    top = jnp.maximum(row_high, row_high_b)
    factor = jnp.exp(row_high - top)
    factor_b = jnp.exp(row_high_b - top)
    total = row_sum * factor + row_sum_b * factor_b
    mixed = jnp.dot(exps.astype(BF16), outs, preferred_element_type=F32) * (factor / total)[:, None]
    mixed += jnp.dot(exps_b, outs_b, preferred_element_type=F32) * (factor_b / total)[:, None]
    return (feats.astype(F32) + mixed).astype(BF16)[None]


def solution(mesh):
    fine = Mesh(mesh.devices.reshape(2, 8, 2, 8, 2), ("xlo", "y", "xhi", "z", "core"))
    grp, seq = ("xlo", "y"), ("xhi", "z", "core")
    in_specs = (P(grp, seq, None), P(grp, None), P(seq, None), P(seq, None, grp), P(seq, grp, None))
    return jax.shard_map(
        local, mesh=fine, in_specs=in_specs, out_specs=P(grp, seq, None), check_vma=False
    )
```

```python
import functools

import jax
import jax.numpy as jnp
from jax import lax
from jax.experimental import pallas as pl
from jax.experimental.pallas import tpu as pltpu
from jax.sharding import Mesh, PartitionSpec as P

F32 = jnp.float32
BF16 = jnp.bfloat16
EXTRA = 128
VMEM = pl.BlockSpec(memory_space=pltpu.VMEM)
ANY = pl.BlockSpec(memory_space=pl.ANY)


def other(length=2):
    return [(k, k ^ 1) for k in range(length)]


def kernel_call(body, outs, flops, moved, specs, *args):
    return pl.pallas_call(
        body,
        out_shape=outs,
        in_specs=specs,
        out_specs=jax.tree.map(lambda _: VMEM, outs),
        compiler_params=pltpu.CompilerParams(vmem_limit_bytes=16 * 2**20),
        cost_estimate=pl.CostEstimate(flops=flops, bytes_accessed=moved, transcendentals=0),
    )(*args)


def split_off(value):
    wide = value * 65537.0
    return wide - (wide - value)


def in_lanes(columns):
    lane = lax.broadcasted_iota(jnp.int32, columns[0].shape, 1)
    packed = jnp.zeros(columns[0].shape, F32)
    for k, column in enumerate(columns):
        first = split_off(column)
        second = split_off(column - first)
        for j, piece in enumerate((first, second, column - first - second)):
            packed = jnp.where(lane == 3 * k + j, piece, packed)
    return packed.astype(BF16)


def dispatch_kernel(own_ref, partner_ref, columns_ref, dummy_ref, message_ref, own_logits_ref, partner_logits_ref):
    width = own_ref.shape[1]
    slots = columns_ref.shape[1]
    columns = columns_ref[...]
    for feats, logits_ref in ((own_ref, own_logits_ref), (partner_ref, partner_logits_ref)):
        logits_ref[...] = jnp.dot(feats[...], columns, preferred_element_type=F32)
    own_logits, partner_logits = own_logits_ref[...], partner_logits_ref[...]
    high = jnp.maximum(
        jnp.max(own_logits, axis=0, keepdims=True), jnp.max(partner_logits, axis=0, keepdims=True)
    )
    own = jnp.exp(own_logits - high).astype(BF16).T
    partner = jnp.exp(partner_logits - high).astype(BF16).T
    step = 512
    for start in range(0, width, step):
        part = slice(start, start + step)
        sums = jnp.dot(own, own_ref[:, part], preferred_element_type=F32)
        sums += jnp.dot(partner, partner_ref[:, part], preferred_element_type=F32)
        message_ref[:, part] = sums.astype(BF16)
    message_ref[:, width:] = in_lanes([jnp.broadcast_to(high, (EXTRA, slots)).T])


def softmax_kernel(own_logits_ref, partner_logits_ref, own_ref, answer_ref):
    for logits_ref, out_ref in ((own_logits_ref, own_ref), (partner_logits_ref, answer_ref)):
        logits = logits_ref[...]
        slots = logits.shape[1]
        high = jnp.max(logits, axis=1, keepdims=True)
        exps = jnp.exp(logits - high)
        total = jnp.sum(exps, axis=1, keepdims=True)
        out_ref[:, :slots] = exps.astype(BF16)
        lanes = (logits.shape[0], EXTRA)
        out_ref[:, slots:] = in_lanes([jnp.broadcast_to(high, lanes), jnp.broadcast_to(total, lanes)])


def pool_kernel(received_ref, gain_ref, slots_ref):
    width = gain_ref.shape[1]
    highs = jnp.sum(received_ref[:, :, width:].astype(F32), axis=-1, keepdims=True)
    overall = jnp.max(highs, axis=0, keepdims=True)
    scale = jnp.exp(highs - overall)
    pooled = received_ref[0, :, :width].astype(F32) * scale[0]
    for k in range(1, received_ref.shape[0]):
        pooled += received_ref[k, :, :width].astype(F32) * scale[k]
    mean_sq = jnp.mean(pooled * pooled, axis=-1, keepdims=True)
    slots = (pooled * lax.rsqrt(mean_sq + 1e-06) * gain_ref[...]).astype(BF16)
    for k in range(slots_ref.shape[0]):
        slots_ref[k] = slots


def expert_kernel(rows_ref, in_ref, early_ref, late_ref, out_ref, out_b_ref, partial_ref):
    rows = rows_ref[...].reshape(-1, rows_ref.shape[-1])
    hidden = jax.nn.gelu(jnp.dot(rows, in_ref[...], preferred_element_type=F32)).astype(BF16)
    cut = early_ref.shape[0]
    summed = jnp.dot(rows[:, :cut], early_ref[...], preferred_element_type=F32)
    summed += jnp.dot(rows[:, cut:], late_ref[...], preferred_element_type=F32)
    hidden_b = jax.nn.gelu(summed).astype(BF16)
    step = 512
    for start in range(0, rows.shape[1], step):
        part = slice(start, start + step)
        sums = jnp.dot(hidden, out_ref[:, part], preferred_element_type=F32)
        sums += jnp.dot(hidden_b, out_b_ref[:, part], preferred_element_type=F32)
        partial_ref[:, :, part] = sums.astype(BF16).reshape(*rows_ref.shape[:2], step)


def sum_kernel(blocks_ref, copies_ref):
    total = blocks_ref[0].astype(F32)
    for k in range(1, blocks_ref.shape[0]):
        total += blocks_ref[k].astype(F32)
    total = total.astype(BF16)
    for k in range(copies_ref.shape[0]):
        copies_ref[k] = total


def piece_sum(block, which):
    part = block[:, 3 * which : 3 * which + 3].astype(F32)
    return part[:, 0] + part[:, 1] + part[:, 2]


def sent_to_all(value, axes):
    length = lax.axis_size(axes)
    return lax.all_to_all(
        jnp.broadcast_to(value[None], (length, *value.shape)), axes, 0, 0, tiled=True
    )


def local(tokens, router, norm_gain, w_in, w_out):
    feats = tokens[0]
    count, width = feats.shape
    slot_count = router.shape[1]
    owners = lax.axis_size(("xhi", "z"))
    groups = lax.axis_size("y")
    per_owner = slot_count // (2 * owners)
    half = slot_count // 2
    core = lax.axis_index("core")
    hidden_units = w_in.shape[2]
    shape = jax.ShapeDtypeStruct

    cut = width * 2 // 3
    partner_early = lax.ppermute(w_in[0, :cut], "xlo", other())
    partner_late = lax.ppermute(w_in[0, cut:], "xlo", other())
    partner_out = lax.ppermute(w_out[0], "xlo", other())
    partner_feats = lax.ppermute(feats, "core", other())

    row = lax.broadcasted_iota(jnp.int32, (slot_count, half), 0)
    col = lax.broadcasted_iota(jnp.int32, (slot_count, half), 1)
    wanted = (col // per_owner * 2 + core) * per_owner + col % per_owner
    pick = (row == wanted).astype(BF16)
    own_columns = jnp.dot(router, pick, preferred_element_type=F32).astype(BF16)
    columns = sent_to_all(own_columns, ("xlo", "y")).reshape(width, half)

    message, logits, partner_logits = kernel_call(
        dispatch_kernel,
        (shape((half, width + EXTRA), BF16), shape((count, half), F32), shape((count, half), F32)),
        8 * count * width * half,
        2 * (2 * count * width + 2 * width * half),
        [VMEM, VMEM, VMEM, ANY],
        feats,
        partner_feats,
        columns,
        partner_early,
    )
    received = lax.all_to_all(
        message.reshape(owners, per_owner, width + EXTRA), ("xhi", "z"), 0, 0, tiled=True
    )

    weights, answer = kernel_call(
        softmax_kernel,
        (shape((count, half + EXTRA), BF16), shape((count, half + EXTRA), BF16)),
        16 * count * half,
        12 * count * half,
        [VMEM] * 2,
        logits,
        partner_logits,
    )
    weights_b = lax.ppermute(answer, "core", other())

    slots = kernel_call(
        pool_kernel,
        shape((groups, per_owner, width), BF16),
        4 * half * width,
        2 * half * width,
        [VMEM] * 2,
        received,
        norm_gain,
    )
    rows = lax.all_to_all(slots, "y", 0, 0, tiled=True)
    partial = kernel_call(
        expert_kernel,
        shape((groups, per_owner, width), BF16),
        8 * groups * per_owner * width * hidden_units,
        8 * width * hidden_units,
        [VMEM] * 6,
        rows,
        w_in[0],
        partner_early,
        partner_late,
        w_out[0],
        partner_out,
    )
    blocks = lax.all_to_all(partial, "y", 0, 0, tiled=True)
    copies = kernel_call(
        sum_kernel,
        shape((owners, per_owner, width), BF16),
        groups * per_owner * width,
        2 * half * width,
        [VMEM],
        blocks,
    )
    outs = lax.all_to_all(copies, ("xhi", "z"), 0, 0, tiled=True).reshape(half, width)
    outs_b = lax.ppermute(outs, "core", other())

    stats, stats_b = weights[:, half:], weights_b[:, half:]
    row_high, row_sum = piece_sum(stats, 0), piece_sum(stats, 1)
    row_high_b, row_sum_b = piece_sum(stats_b, 0), piece_sum(stats_b, 1)
    top = jnp.maximum(row_high, row_high_b)
    factor = jnp.exp(row_high - top)
    factor_b = jnp.exp(row_high_b - top)
    total = row_sum * factor + row_sum_b * factor_b
    mixed = jnp.dot(weights[:, :half], outs, preferred_element_type=F32) * (factor / total)[:, None]
    mixed += jnp.dot(weights_b[:, :half], outs_b, preferred_element_type=F32) * (factor_b / total)[:, None]
    return (feats.astype(F32) + mixed).astype(BF16)[None]


def solution(mesh):
    fine = Mesh(mesh.devices.reshape(2, 8, 2, 8, 2), ("xlo", "y", "xhi", "z", "core"))
    grp, seq = ("xlo", "y"), ("xhi", "z", "core")
    in_specs = (P(grp, seq, None), P(grp, None), P(seq, None), P(seq, None, grp), P(seq, grp, None))
    return jax.shard_map(
        local, mesh=fine, in_specs=in_specs, out_specs=P(grp, seq, None), check_vma=False
    )
```

```python
import jax
import jax.numpy as jnp
from jax import lax
from jax.experimental import pallas as pl
from jax.experimental.pallas import tpu as pltpu
from jax.sharding import Mesh, PartitionSpec as P

F32 = jnp.float32
BF16 = jnp.bfloat16
EXTRA = 128
VMEM = pl.BlockSpec(memory_space=pltpu.VMEM)
HBM = pl.BlockSpec(memory_space=pltpu.HBM)


def other(length=2):
    return [(k, k ^ 1) for k in range(length)]


def kernel_call(body, outs, flops, moved, specs, *args, out_specs=None, scratch=(), room=60):
    return pl.pallas_call(
        body,
        out_shape=outs,
        in_specs=specs,
        out_specs=jax.tree.map(lambda _: VMEM, outs) if out_specs is None else out_specs,
        scratch_shapes=scratch,
        compiler_params=pltpu.CompilerParams(vmem_limit_bytes=room * 2**20),
        cost_estimate=pl.CostEstimate(flops=flops, bytes_accessed=moved, transcendentals=0),
    )(*args)


def started(source, target, semaphores, k):
    copy = pltpu.make_async_copy(source, target, semaphores.at[k])
    copy.start()
    return copy


def split_off(value):
    wide = value * 65537.0
    return wide - (wide - value)


def in_lanes(columns):
    lane = lax.broadcasted_iota(jnp.int32, columns[0].shape, 1)
    packed = jnp.zeros(columns[0].shape, F32)
    for k, column in enumerate(columns):
        first = split_off(column)
        second = split_off(column - first)
        for j, piece in enumerate((first, second, column - first - second)):
            packed = jnp.where(lane == 3 * k + j, piece, packed)
    return packed.astype(BF16)


def dispatch_kernel(
    own_hbm,
    partner_hbm,
    columns_ref,
    message_ref,
    own_logits_hbm,
    partner_logits_hbm,
    own_ref,
    partner_ref,
    own_logits_ref,
    partner_logits_ref,
    semaphores,
):
    width = own_ref.shape[1]
    slots = columns_ref.shape[1]
    loads = [
        started(own_hbm, own_ref, semaphores, 0),
        started(partner_hbm, partner_ref, semaphores, 1),
    ]
    columns = columns_ref[...]
    loads[0].wait()
    own_logits_ref[...] = jnp.dot(own_ref[...], columns, preferred_element_type=F32)
    stores = [started(own_logits_ref, own_logits_hbm, semaphores, 2)]
    loads[1].wait()
    partner_logits_ref[...] = jnp.dot(partner_ref[...], columns, preferred_element_type=F32)
    stores.append(started(partner_logits_ref, partner_logits_hbm, semaphores, 3))
    own_logits, partner_logits = own_logits_ref[...], partner_logits_ref[...]
    high = jnp.maximum(
        jnp.max(own_logits, axis=0, keepdims=True), jnp.max(partner_logits, axis=0, keepdims=True)
    )
    own = jnp.exp(own_logits - high).astype(BF16).T
    partner = jnp.exp(partner_logits - high).astype(BF16).T
    step = 512
    for start in range(0, width, step):
        part = slice(start, start + step)
        sums = jnp.dot(own, own_ref[:, part], preferred_element_type=F32)
        sums += jnp.dot(partner, partner_ref[:, part], preferred_element_type=F32)
        message_ref[:, part] = sums.astype(BF16)
    message_ref[:, width:] = in_lanes([jnp.broadcast_to(high, (EXTRA, slots)).T])
    for copy in stores:
        copy.wait()


def softmax_kernel(own_logits_ref, partner_logits_ref, own_ref, answer_ref):
    for logits_ref, out_ref in ((own_logits_ref, own_ref), (partner_logits_ref, answer_ref)):
        logits = logits_ref[...]
        slots = logits.shape[1]
        high = jnp.max(logits, axis=1, keepdims=True)
        exps = jnp.exp(logits - high)
        total = jnp.sum(exps, axis=1, keepdims=True)
        out_ref[:, :slots] = exps.astype(BF16)
        lanes = (logits.shape[0], EXTRA)
        out_ref[:, slots:] = in_lanes([jnp.broadcast_to(high, lanes), jnp.broadcast_to(total, lanes)])


def pool_kernel(received_ref, gain_ref, slots_ref):
    width = gain_ref.shape[1]
    highs = jnp.sum(received_ref[:, :, width:].astype(F32), axis=-1, keepdims=True)
    overall = jnp.max(highs, axis=0, keepdims=True)
    scale = jnp.exp(highs - overall)
    pooled = received_ref[0, :, :width].astype(F32) * scale[0]
    for k in range(1, received_ref.shape[0]):
        pooled += received_ref[k, :, :width].astype(F32) * scale[k]
    mean_sq = jnp.mean(pooled * pooled, axis=-1, keepdims=True)
    slots = (pooled * lax.rsqrt(mean_sq + 1e-06) * gain_ref[...]).astype(BF16)
    for k in range(slots_ref.shape[0]):
        slots_ref[k] = slots


def pack_kernel(in_hbm, out_hbm, packed_hbm, semaphores):
    rows, units = in_hbm.shape
    copies = [started(in_hbm, packed_hbm.at[pl.ds(0, rows)], semaphores, 0)]
    for k in range(rows // units):
        block = out_hbm.at[:, pl.ds(k * units, units)]
        copies.append(started(block, packed_hbm.at[pl.ds(rows + k * units, units)], semaphores, k + 1))
    for copy in copies:
        copy.wait()


def expert_kernel(
    rows_ref, in_hbm, out_hbm, packed_hbm, partial_ref, in_ref, out_ref, in_b_ref, out_b_ref, semaphores
):
    rows = rows_ref[...].reshape(-1, rows_ref.shape[-1])
    width, units = in_ref.shape
    loads = [
        started(in_hbm, in_ref, semaphores, 0),
        started(packed_hbm.at[pl.ds(0, width)], in_b_ref, semaphores, 1),
        started(out_hbm, out_ref, semaphores, 2),
        started(packed_hbm.at[pl.ds(width, width)], out_b_ref, semaphores, 3),
    ]
    loads[0].wait()
    hidden = jax.nn.gelu(jnp.dot(rows, in_ref[...], preferred_element_type=F32)).astype(BF16)
    loads[1].wait()
    hidden_b = jax.nn.gelu(jnp.dot(rows, in_b_ref[...], preferred_element_type=F32)).astype(BF16)
    loads[2].wait()
    loads[3].wait()
    for start in range(0, width, units):
        part = slice(start, start + units)
        sums = jnp.dot(hidden, out_ref[:, part], preferred_element_type=F32)
        sums += jnp.dot(hidden_b, out_b_ref[part, :], preferred_element_type=F32)
        partial_ref[:, :, part] = sums.astype(BF16).reshape(*rows_ref.shape[:2], units)


def sum_kernel(blocks_ref, copies_hbm, total_ref, semaphores):
    total = blocks_ref[0].astype(F32)
    for k in range(1, blocks_ref.shape[0]):
        total += blocks_ref[k].astype(F32)
    total_ref[...] = total.astype(BF16)
    copies = [started(total_ref, copies_hbm.at[k], semaphores, k) for k in range(copies_hbm.shape[0])]
    for copy in copies:
        copy.wait()


def piece_sum(block, which):
    part = block[:, 3 * which : 3 * which + 3].astype(F32)
    return part[:, 0] + part[:, 1] + part[:, 2]


def sent_to_all(value, axes):
    length = lax.axis_size(axes)
    return lax.all_to_all(
        jnp.broadcast_to(value[None], (length, *value.shape)), axes, 0, 0, tiled=True
    )


def local(tokens, router, norm_gain, w_in, w_out):
    feats = tokens[0]
    count, width = feats.shape
    slot_count = router.shape[1]
    owners = lax.axis_size(("xhi", "z"))
    groups = lax.axis_size("y")
    per_owner = slot_count // (2 * owners)
    half = slot_count // 2
    core = lax.axis_index("core")
    hidden_units = w_in.shape[2]
    shape = jax.ShapeDtypeStruct

    packed = kernel_call(
        pack_kernel,
        shape((2 * width, hidden_units), BF16),
        0,
        8 * width * hidden_units,
        [HBM] * 2,
        w_in[0],
        w_out[0],
        out_specs=HBM,
        scratch=[pltpu.SemaphoreType.DMA((1 + width // hidden_units,))],
    )
    partner_packed = lax.ppermute(packed, "xlo", other())
    partner_feats = lax.ppermute(feats, "core", other())

    row = lax.broadcasted_iota(jnp.int32, (slot_count, half), 0)
    col = lax.broadcasted_iota(jnp.int32, (slot_count, half), 1)
    wanted = (col // per_owner * 2 + core) * per_owner + col % per_owner
    pick = (row == wanted).astype(BF16)
    own_columns = jnp.dot(router, pick, preferred_element_type=F32).astype(BF16)
    columns = sent_to_all(own_columns, ("xlo", "y")).reshape(width, half)

    message, logits, partner_logits = kernel_call(
        dispatch_kernel,
        (shape((half, width + EXTRA), BF16), shape((count, half), F32), shape((count, half), F32)),
        8 * count * width * half,
        2 * (2 * count * width + 2 * width * half),
        [HBM, HBM, VMEM],
        feats,
        partner_feats,
        columns,
        out_specs=(VMEM, HBM, HBM),
        scratch=[
            pltpu.VMEM((count, width), BF16),
            pltpu.VMEM((count, width), BF16),
            pltpu.VMEM((count, half), F32),
            pltpu.VMEM((count, half), F32),
            pltpu.SemaphoreType.DMA((4,)),
        ],
    )
    received = lax.all_to_all(
        message.reshape(owners, per_owner, width + EXTRA), ("xhi", "z"), 0, 0, tiled=True
    )

    weights, answer = kernel_call(
        softmax_kernel,
        (shape((count, half + EXTRA), BF16), shape((count, half + EXTRA), BF16)),
        16 * count * half,
        12 * count * half,
        [VMEM] * 2,
        logits,
        partner_logits,
    )
    weights_b = lax.ppermute(answer, "core", other())

    slots = kernel_call(
        pool_kernel,
        shape((groups, per_owner, width), BF16),
        4 * half * width,
        2 * half * width,
        [VMEM] * 2,
        received,
        norm_gain,
        room=16,
    )
    rows = lax.all_to_all(slots, "y", 0, 0, tiled=True)
    partial = kernel_call(
        expert_kernel,
        shape((groups, per_owner, width), BF16),
        8 * groups * per_owner * width * hidden_units,
        8 * width * hidden_units,
        [VMEM, HBM, HBM, HBM],
        rows,
        w_in[0],
        w_out[0],
        partner_packed,
        scratch=[
            pltpu.VMEM((width, hidden_units), BF16),
            pltpu.VMEM((hidden_units, width), BF16),
            pltpu.VMEM((width, hidden_units), BF16),
            pltpu.VMEM((width, hidden_units), BF16),
            pltpu.SemaphoreType.DMA((4,)),
        ],
        room=48,
    )
    blocks = lax.all_to_all(partial, "y", 0, 0, tiled=True)
    copies = kernel_call(
        sum_kernel,
        shape((owners, per_owner, width), BF16),
        groups * per_owner * width,
        2 * half * width,
        [VMEM],
        blocks,
        out_specs=HBM,
        scratch=[pltpu.VMEM((per_owner, width), BF16), pltpu.SemaphoreType.DMA((owners,))],
        room=16,
    )
    outs = lax.all_to_all(copies, ("xhi", "z"), 0, 0, tiled=True).reshape(half, width)
    outs_b = lax.ppermute(outs, "core", other())

    stats, stats_b = weights[:, half:], weights_b[:, half:]
    row_high, row_sum = piece_sum(stats, 0), piece_sum(stats, 1)
    row_high_b, row_sum_b = piece_sum(stats_b, 0), piece_sum(stats_b, 1)
    top = jnp.maximum(row_high, row_high_b)
    factor = jnp.exp(row_high - top)
    factor_b = jnp.exp(row_high_b - top)
    total = row_sum * factor + row_sum_b * factor_b
    mixed = jnp.dot(weights[:, :half], outs, preferred_element_type=F32) * (factor / total)[:, None]
    mixed += jnp.dot(weights_b[:, :half], outs_b, preferred_element_type=F32) * (factor_b / total)[:, None]
    return (feats.astype(F32) + mixed).astype(BF16)[None]


def solution(mesh):
    fine = Mesh(mesh.devices.reshape(2, 8, 2, 8, 2), ("xlo", "y", "xhi", "z", "core"))
    grp, seq = ("xlo", "y"), ("xhi", "z", "core")
    in_specs = (P(grp, seq, None), P(grp, None), P(seq, None), P(seq, None, grp), P(seq, grp, None))
    return jax.shard_map(
        local, mesh=fine, in_specs=in_specs, out_specs=P(grp, seq, None), check_vma=False
    )
```

```python
import jax
import jax.numpy as jnp
from jax import lax
from jax.experimental import pallas as pl
from jax.experimental.pallas import tpu as pltpu
from jax.sharding import Mesh, PartitionSpec as P

F32 = jnp.float32
BF16 = jnp.bfloat16
EXTRA = 128
VMEM = pl.BlockSpec(memory_space=pltpu.VMEM)
HBM = pl.BlockSpec(memory_space=pltpu.HBM)


def other(length=2):
    return [(k, k ^ 1) for k in range(length)]


def kernel_call(body, outs, flops, moved, specs, *args, out_specs=None, scratch=(), room=60):
    return pl.pallas_call(
        body,
        out_shape=outs,
        in_specs=specs,
        out_specs=jax.tree.map(lambda _: VMEM, outs) if out_specs is None else out_specs,
        scratch_shapes=scratch,
        compiler_params=pltpu.CompilerParams(vmem_limit_bytes=int(room * 2**20)),
        cost_estimate=pl.CostEstimate(flops=flops, bytes_accessed=moved, transcendentals=0),
    )(*args)


def started(source, target, semaphores, k):
    copy = pltpu.make_async_copy(source, target, semaphores.at[k])
    copy.start()
    return copy


def started_rows(source, target, semaphores, first, count):
    rows = source.shape[0] // count
    parts = [pl.ds(k * rows, rows) for k in range(count)]
    return [started(source.at[p], target.at[p], semaphores, first + k) for k, p in enumerate(parts)]


def split_off(value):
    wide = value * 65537.0
    return wide - (wide - value)


def in_lanes(columns):
    lane = lax.broadcasted_iota(jnp.int32, columns[0].shape, 1)
    packed = jnp.zeros(columns[0].shape, F32)
    for k, column in enumerate(columns):
        first = split_off(column)
        second = split_off(column - first)
        for j, piece in enumerate((first, second, column - first - second)):
            packed = jnp.where(lane == 3 * k + j, piece, packed)
    return packed.astype(BF16)


def dispatch_kernel(
    own_hbm,
    partner_hbm,
    columns_hbm,
    message_hbm,
    own_logits_hbm,
    partner_logits_hbm,
    own_ref,
    partner_ref,
    columns_ref,
    own_logits_ref,
    partner_logits_ref,
    message_ref,
    semaphores,
):
    width = own_ref.shape[1]
    slots = columns_ref.shape[1]
    cuts = 4
    first = started_rows(columns_hbm, columns_ref, semaphores, 15, cuts)
    loads = started_rows(own_hbm, own_ref, semaphores, 0, cuts)
    loads += started_rows(partner_hbm, partner_ref, semaphores, cuts, cuts)
    for copy in first + loads[:cuts]:
        copy.wait()
    columns = columns_ref[...]
    own_logits_ref[...] = jnp.dot(own_ref[...], columns, preferred_element_type=F32)
    stores = [started(own_logits_ref, own_logits_hbm, semaphores, 2 * cuts)]
    for copy in loads[cuts:]:
        copy.wait()
    partner_logits_ref[...] = jnp.dot(partner_ref[...], columns, preferred_element_type=F32)
    stores.append(started(partner_logits_ref, partner_logits_hbm, semaphores, 2 * cuts + 1))
    own_logits, partner_logits = own_logits_ref[...], partner_logits_ref[...]
    high = jnp.maximum(
        jnp.max(own_logits, axis=0, keepdims=True), jnp.max(partner_logits, axis=0, keepdims=True)
    )
    message_ref[:, width:] = in_lanes([jnp.broadcast_to(high, (EXTRA, slots)).T])
    last = pl.ds(width, EXTRA)
    stores.append(started(message_ref.at[:, last], message_hbm.at[:, last], semaphores, 2 * cuts + 2))
    own = jnp.exp(own_logits - high).astype(BF16).T
    partner = jnp.exp(partner_logits - high).astype(BF16).T
    step = 384
    for k in range(width // step):
        part = pl.ds(k * step, step)
        sums = jnp.dot(own, own_ref[:, part], preferred_element_type=F32)
        sums += jnp.dot(partner, partner_ref[:, part], preferred_element_type=F32)
        message_ref[:, part] = sums.astype(BF16)
        stores.append(started(message_ref.at[:, part], message_hbm.at[:, part], semaphores, 2 * cuts + 3 + k))
    for copy in stores:
        copy.wait()


def softmax_kernel(own_logits_ref, partner_logits_ref, own_ref, answer_ref):
    for logits_ref, out_ref in ((own_logits_ref, own_ref), (partner_logits_ref, answer_ref)):
        logits = logits_ref[...]
        slots = logits.shape[1]
        high = jnp.max(logits, axis=1, keepdims=True)
        exps = jnp.exp(logits - high)
        total = jnp.sum(exps, axis=1, keepdims=True)
        out_ref[:, :slots] = exps.astype(BF16)
        lanes = (logits.shape[0], EXTRA)
        out_ref[:, slots:] = in_lanes([jnp.broadcast_to(high, lanes), jnp.broadcast_to(total, lanes)])


def pool_kernel(received_ref, gain_ref, copies_hbm, slots_ref, semaphores):
    width = gain_ref.shape[1]
    highs = jnp.sum(received_ref[:, :, width:].astype(F32), axis=-1, keepdims=True)
    overall = jnp.max(highs, axis=0, keepdims=True)
    scale = jnp.exp(highs - overall)
    pooled = received_ref[0, :, :width].astype(F32) * scale[0]
    for k in range(1, received_ref.shape[0]):
        pooled += received_ref[k, :, :width].astype(F32) * scale[k]
    mean_sq = jnp.mean(pooled * pooled, axis=-1, keepdims=True)
    slots_ref[...] = (pooled * lax.rsqrt(mean_sq + 1e-06) * gain_ref[...]).astype(BF16)
    copies = [started(slots_ref, copies_hbm.at[k], semaphores, k) for k in range(copies_hbm.shape[0])]
    for copy in copies:
        copy.wait()


def follow_kernel(weights_hbm, before_hbm, weights_ref, semaphores):
    for copy in started_rows(weights_hbm, weights_ref, semaphores, 0, semaphores.shape[0]):
        copy.wait()


def expert_kernel(
    rows_ref,
    in_hbm,
    out_hbm,
    in_b_hbm,
    out_b_hbm,
    partial_ref,
    in_ref,
    out_ref,
    in_b_ref,
    out_b_ref,
    semaphores,
):
    rows = rows_ref[...].reshape(-1, rows_ref.shape[-1])
    width = rows.shape[1]
    cuts = 4
    pairs = ((in_hbm, in_ref), (in_b_hbm, in_b_ref), (out_hbm, out_ref), (out_b_hbm, out_b_ref))
    loads = [started_rows(*pair, semaphores, cuts * k, cuts) for k, pair in enumerate(pairs)]
    for copy in loads[0]:
        copy.wait()
    hidden = jax.nn.gelu(jnp.dot(rows, in_ref[...], preferred_element_type=F32)).astype(BF16)
    for copy in loads[1]:
        copy.wait()
    hidden_b = jax.nn.gelu(jnp.dot(rows, in_b_ref[...], preferred_element_type=F32)).astype(BF16)
    for copy in loads[2] + loads[3]:
        copy.wait()
    step = 512
    for k in range(width // step):
        part = pl.ds(k * step, step)
        sums = jnp.dot(hidden, out_ref[:, part], preferred_element_type=F32)
        sums += jnp.dot(hidden_b, out_b_ref[:, part], preferred_element_type=F32)
        partial_ref[:, :, part] = sums.astype(BF16).reshape(*rows_ref.shape[:2], step)


def sum_kernel(blocks_ref, copies_hbm, total_ref, semaphores):
    total = blocks_ref[0].astype(F32)
    for k in range(1, blocks_ref.shape[0]):
        total += blocks_ref[k].astype(F32)
    total_ref[...] = total.astype(BF16)
    copies = [started(total_ref, copies_hbm.at[k], semaphores, k) for k in range(copies_hbm.shape[0])]
    for copy in copies:
        copy.wait()


def piece_sum(block, which):
    part = block[:, 3 * which : 3 * which + 3].astype(F32)
    return part[:, 0] + part[:, 1] + part[:, 2]


def sent_to_all(value, axes):
    length = lax.axis_size(axes)
    return lax.all_to_all(
        jnp.broadcast_to(value[None], (length, *value.shape)), axes, 0, 0, tiled=True
    )


def local(tokens, router, norm_gain, w_in, w_out):
    feats = tokens[0]
    count, width = feats.shape
    slot_count = router.shape[1]
    owners = lax.axis_size(("xhi", "z"))
    groups = lax.axis_size("y")
    per_owner = slot_count // (2 * owners)
    half = slot_count // 2
    core = lax.axis_index("core")
    hidden_units = w_in.shape[2]
    shape = jax.ShapeDtypeStruct

    partner_in = lax.ppermute(w_in[0], "xlo", other())
    out_later = kernel_call(
        follow_kernel,
        shape((hidden_units, width), BF16),
        0,
        4 * width * hidden_units,
        [HBM] * 2,
        w_out[0],
        partner_in,
        scratch=[pltpu.SemaphoreType.DMA((4,))],
        room=16,
    )
    partner_out = lax.ppermute(out_later, "xlo", other())
    partner_feats = lax.ppermute(feats, "core", other())

    row = lax.broadcasted_iota(jnp.int32, (slot_count, half), 0)
    col = lax.broadcasted_iota(jnp.int32, (slot_count, half), 1)
    wanted = (col // per_owner * 2 + core) * per_owner + col % per_owner
    pick = (row == wanted).astype(BF16)
    own_columns = jnp.dot(router, pick, preferred_element_type=F32).astype(BF16)
    columns = sent_to_all(own_columns, ("xlo", "y")).reshape(width, half)

    message, logits, partner_logits = kernel_call(
        dispatch_kernel,
        (shape((half, width + EXTRA), BF16), shape((count, half), F32), shape((count, half), F32)),
        8 * count * width * half,
        2 * (2 * count * width + 2 * width * half),
        [HBM] * 3,
        feats,
        partner_feats,
        columns,
        out_specs=(HBM, HBM, HBM),
        scratch=[
            pltpu.VMEM((count, width), BF16),
            pltpu.VMEM((count, width), BF16),
            pltpu.VMEM((width, half), BF16),
            pltpu.VMEM((count, half), F32),
            pltpu.VMEM((count, half), F32),
            pltpu.VMEM((half, width + EXTRA), BF16),
            pltpu.SemaphoreType.DMA((19,)),
        ],
        room=58,
    )
    received = lax.all_to_all(
        message.reshape(owners, per_owner, width + EXTRA), ("xhi", "z"), 0, 0, tiled=True
    )

    weights, answer = kernel_call(
        softmax_kernel,
        (shape((count, half + EXTRA), BF16), shape((count, half + EXTRA), BF16)),
        16 * count * half,
        12 * count * half,
        [VMEM] * 2,
        logits,
        partner_logits,
    )
    weights_b = lax.ppermute(answer, "core", other())

    slots = kernel_call(
        pool_kernel,
        shape((groups, per_owner, width), BF16),
        4 * half * width,
        2 * half * width,
        [VMEM] * 2,
        received,
        norm_gain,
        out_specs=HBM,
        scratch=[pltpu.VMEM((per_owner, width), BF16), pltpu.SemaphoreType.DMA((groups,))],
        room=16,
    )
    rows = lax.all_to_all(slots, "y", 0, 0, tiled=True)
    partial = kernel_call(
        expert_kernel,
        shape((groups, per_owner, width), BF16),
        8 * groups * per_owner * width * hidden_units,
        8 * width * hidden_units,
        [VMEM, HBM, HBM, HBM, HBM],
        rows,
        w_in[0],
        w_out[0],
        partner_in,
        partner_out,
        scratch=[
            pltpu.VMEM((width, hidden_units), BF16),
            pltpu.VMEM((hidden_units, width), BF16),
            pltpu.VMEM((width, hidden_units), BF16),
            pltpu.VMEM((hidden_units, width), BF16),
            pltpu.SemaphoreType.DMA((16,)),
        ],
        room=48,
    )
    blocks = lax.all_to_all(partial, "y", 0, 0, tiled=True)
    copies = kernel_call(
        sum_kernel,
        shape((owners, per_owner, width), BF16),
        groups * per_owner * width,
        2 * half * width,
        [VMEM],
        blocks,
        out_specs=HBM,
        scratch=[pltpu.VMEM((per_owner, width), BF16), pltpu.SemaphoreType.DMA((owners,))],
        room=16,
    )
    outs = lax.all_to_all(copies, ("xhi", "z"), 0, 0, tiled=True).reshape(half, width)
    outs_b = lax.ppermute(outs, "core", other())

    stats, stats_b = weights[:, half:], weights_b[:, half:]
    row_high, row_sum = piece_sum(stats, 0), piece_sum(stats, 1)
    row_high_b, row_sum_b = piece_sum(stats_b, 0), piece_sum(stats_b, 1)
    top = jnp.maximum(row_high, row_high_b)
    factor = jnp.exp(row_high - top)
    factor_b = jnp.exp(row_high_b - top)
    total = row_sum * factor + row_sum_b * factor_b
    mixed = jnp.dot(weights[:, :half], outs, preferred_element_type=F32) * (factor / total)[:, None]
    mixed += jnp.dot(weights_b[:, :half], outs_b, preferred_element_type=F32) * (factor_b / total)[:, None]
    return (feats.astype(F32) + mixed).astype(BF16)[None]


def solution(mesh):
    fine = Mesh(mesh.devices.reshape(2, 8, 2, 8, 2), ("xlo", "y", "xhi", "z", "core"))
    grp, seq = ("xlo", "y"), ("xhi", "z", "core")
    in_specs = (P(grp, seq, None), P(grp, None), P(seq, None), P(seq, None, grp), P(seq, grp, None))
    return jax.shard_map(
        local, mesh=fine, in_specs=in_specs, out_specs=P(grp, seq, None), check_vma=False
    )
```

```python
import jax
import jax.numpy as jnp
from jax import lax
from jax.experimental import pallas as pl
from jax.experimental.pallas import tpu as pltpu
from jax.sharding import Mesh, PartitionSpec as P

F32 = jnp.float32
BF16 = jnp.bfloat16
EXTRA = 128
Z = ("zh", "zl")
VMEM = pl.BlockSpec(memory_space=pltpu.VMEM)
HBM = pl.BlockSpec(memory_space=pltpu.HBM)


def other(length=2):
    return [(k, k ^ 1) for k in range(length)]


def kernel_call(body, outs, flops, moved, specs, *args, out_specs=None, scratch=(), room=60):
    return pl.pallas_call(
        body,
        out_shape=outs,
        in_specs=specs,
        out_specs=jax.tree.map(lambda _: VMEM, outs) if out_specs is None else out_specs,
        scratch_shapes=scratch,
        compiler_params=pltpu.CompilerParams(vmem_limit_bytes=int(room * 2**20)),
        cost_estimate=pl.CostEstimate(flops=flops, bytes_accessed=moved, transcendentals=0),
    )(*args)


def started(source, target, semaphores, k):
    copy = pltpu.make_async_copy(source, target, semaphores.at[k])
    copy.start()
    return copy


def started_rows(source, target, semaphores, first, count):
    rows = source.shape[0] // count
    parts = [pl.ds(k * rows, rows) for k in range(count)]
    return [started(source.at[p], target.at[p], semaphores, first + k) for k, p in enumerate(parts)]


def split_off(value):
    wide = value * 65537.0
    return wide - (wide - value)


def in_lanes(columns):
    lane = lax.broadcasted_iota(jnp.int32, columns[0].shape, 1)
    packed = jnp.zeros(columns[0].shape, F32)
    for k, column in enumerate(columns):
        first = split_off(column)
        second = split_off(column - first)
        for j, piece in enumerate((first, second, column - first - second)):
            packed = jnp.where(lane == 3 * k + j, piece, packed)
    return packed.astype(BF16)


def dispatch_kernel(*refs):
    sources, refs = refs[:7], refs[7:]
    message_hbm, logits_hbm, columns_ref, *feats = refs[:9]
    logits_ref, message_ref, semaphores = refs[9:]
    width, slots = columns_ref.shape
    targets = [columns_ref, *feats]
    loads = [started(source, target, semaphores, k) for k, (source, target) in enumerate(zip(sources, targets))]
    loads[0].wait()
    columns = columns_ref[...]
    offset, high, rows = 0, None, []
    for load, feats_ref in zip(loads[1:], feats):
        load.wait()
        part = slice(offset, offset + feats_ref.shape[0])
        logits = jnp.dot(feats_ref[...], columns, preferred_element_type=F32)
        logits_ref[part, :] = logits
        top = jnp.max(logits, axis=0, keepdims=True)
        high = top if high is None else jnp.maximum(high, top)
        offset += feats_ref.shape[0]
        rows.append(part)
    stores = [started(logits_ref, logits_hbm, semaphores, 7)]
    message_ref[:, width:] = in_lanes([jnp.broadcast_to(high, (EXTRA, slots)).T])
    last = pl.ds(width, EXTRA)
    stores.append(started(message_ref.at[:, last], message_hbm.at[:, last], semaphores, 8))
    dispatch = [jnp.exp(logits_ref[part, :] - high).astype(BF16).T for part in rows]
    step = 512
    for k in range(width // step):
        part = pl.ds(k * step, step)
        sums = jnp.dot(dispatch[0], feats[0][:, part], preferred_element_type=F32)
        for one, feats_ref in zip(dispatch[1:], feats[1:]):
            sums += jnp.dot(one, feats_ref[:, part], preferred_element_type=F32)
        message_ref[:, part] = sums.astype(BF16)
        stores.append(started(message_ref.at[:, part], message_hbm.at[:, part], semaphores, 9 + k))
    for copy in stores:
        copy.wait()


def exps_kernel(logits_ref, own_ref, answer_ref):
    rows, slots = own_ref.shape[0], logits_ref.shape[1]
    for k, out_ref in enumerate((own_ref, answer_ref)):
        logits = logits_ref[k * rows : (k + 1) * rows, :]
        high = jnp.max(logits, axis=1, keepdims=True)
        exps = jnp.exp(logits - high)
        total = jnp.sum(exps, axis=1, keepdims=True)
        out_ref[:, :slots] = exps.astype(BF16)
        lanes = (rows, EXTRA)
        out_ref[:, slots:] = in_lanes([jnp.broadcast_to(high, lanes), jnp.broadcast_to(total, lanes)])


def weights_kernel(side_ref, own_ref, core_ref, low_ref, up_ref, own_weights_ref, core_weights_ref):
    rows, wide = low_ref.shape[0] * 2, own_ref.shape[1]
    slots = wide - EXTRA
    half = rows // 2
    side = side_ref[0]
    for k, given_ref in enumerate((low_ref, up_ref)):
        part = slice(k * half, (k + 1) * half)
        blocks = [own_ref[part, :], core_ref[part, :], given_ref[:, :wide], given_ref[:, wide:]]
        lane = lax.broadcasted_iota(jnp.int32, (half, EXTRA), 1)
        stats = [block[:, slots:].astype(F32) for block in blocks]
        highs = [jnp.sum(jnp.where(lane < 3, s, 0.0), axis=1, keepdims=True) for s in stats]
        sums = [jnp.sum(jnp.where(lane < 3, 0.0, s), axis=1, keepdims=True) for s in stats]
        top = jnp.maximum(jnp.maximum(highs[0], highs[1]), jnp.maximum(highs[2], highs[3]))
        factors = [jnp.exp(high - top) for high in highs]
        total = sums[0] * factors[0] + sums[1] * factors[1] + sums[2] * factors[2] + sums[3] * factors[3]
        scaled = [
            (block[:, :slots].astype(F32) * (factor / total)).astype(BF16)
            for block, factor in zip(blocks, factors)
        ]
        here = pl.ds(pl.multiple_of(side * slots, slots), slots)
        there = pl.ds(pl.multiple_of((1 - side) * slots, slots), slots)
        own_weights_ref[part, here] = scaled[0]
        core_weights_ref[part, here] = scaled[1]
        own_weights_ref[part, there] = scaled[2]
        core_weights_ref[part, there] = scaled[3]


def pool_kernel(received_ref, gain_ref, copies_hbm, slots_ref, semaphores):
    width = gain_ref.shape[1]
    highs = jnp.sum(received_ref[:, :, width:].astype(F32), axis=-1, keepdims=True)
    overall = jnp.max(highs, axis=0, keepdims=True)
    scale = jnp.exp(highs - overall)
    pooled = received_ref[0, :, :width].astype(F32) * scale[0]
    for k in range(1, received_ref.shape[0]):
        pooled += received_ref[k, :, :width].astype(F32) * scale[k]
    mean_sq = jnp.mean(pooled * pooled, axis=-1, keepdims=True)
    slots_ref[...] = (pooled * lax.rsqrt(mean_sq + 1e-06) * gain_ref[...]).astype(BF16)
    copies = [started(slots_ref, copies_hbm.at[k], semaphores, k) for k in range(copies_hbm.shape[0])]
    for copy in copies:
        copy.wait()


def follow_kernel(weights_hbm, before_hbm, weights_ref, semaphores):
    for copy in started_rows(weights_hbm, weights_ref, semaphores, 0, semaphores.shape[0]):
        copy.wait()


def expert_kernel(
    rows_ref,
    in_hbm,
    out_hbm,
    in_b_hbm,
    out_b_hbm,
    before_hbm,
    partial_ref,
    in_ref,
    out_ref,
    in_b_ref,
    out_b_ref,
    semaphores,
):
    rows = rows_ref[...].reshape(-1, rows_ref.shape[-1])
    width = rows.shape[1]
    cuts = 4
    pairs = ((in_hbm, in_ref), (in_b_hbm, in_b_ref), (out_hbm, out_ref), (out_b_hbm, out_b_ref))
    loads = [started_rows(*pair, semaphores, cuts * k, cuts) for k, pair in enumerate(pairs)]
    for copy in loads[0]:
        copy.wait()
    hidden = jax.nn.gelu(jnp.dot(rows, in_ref[...], preferred_element_type=F32)).astype(BF16)
    for copy in loads[1]:
        copy.wait()
    hidden_b = jax.nn.gelu(jnp.dot(rows, in_b_ref[...], preferred_element_type=F32)).astype(BF16)
    for copy in loads[2] + loads[3]:
        copy.wait()
    step = 512
    for k in range(width // step):
        part = pl.ds(k * step, step)
        sums = jnp.dot(hidden, out_ref[:, part], preferred_element_type=F32)
        sums += jnp.dot(hidden_b, out_b_ref[:, part], preferred_element_type=F32)
        partial_ref[:, :, part] = sums.astype(BF16).reshape(*rows_ref.shape[:2], step)


def sum_kernel(blocks_ref, before_hbm, copies_hbm, total_ref, semaphores):
    total = blocks_ref[0].astype(F32)
    for k in range(1, blocks_ref.shape[0]):
        total += blocks_ref[k].astype(F32)
    total_ref[...] = total.astype(BF16)
    copies = [started(total_ref, copies_hbm.at[k], semaphores, k) for k in range(copies_hbm.shape[0])]
    for copy in copies:
        copy.wait()


def sent_to_all(value, axes):
    length = lax.axis_size(axes)
    return lax.all_to_all(
        jnp.broadcast_to(value[None], (length, *value.shape)), axes, 0, 0, tiled=True
    )


def local(tokens, router, norm_gain, w_in, w_out):
    feats = tokens[0]
    count, width = feats.shape
    slot_count = router.shape[1]
    depth = lax.axis_size(Z)
    owners = lax.axis_size(("xhi", "zh"))
    groups = lax.axis_size("y")
    per_owner = slot_count // (4 * owners)
    quarter = slot_count // 4
    core, side = lax.axis_index("core"), lax.axis_index("zl")
    hidden_units = w_in.shape[2]
    shape = jax.ShapeDtypeStruct
    up = [(k, (k + 1) % depth) for k in range(depth)]
    down = [(k, (k - 1) % depth) for k in range(depth)]

    middle = count // 2
    above = lax.ppermute(feats[:middle], Z, down)
    below = lax.ppermute(feats[middle:], Z, up)
    mine = [feats, above, below]
    theirs = [lax.ppermute(block, "core", other()) for block in mine]

    row = lax.broadcasted_iota(jnp.int32, (slot_count, quarter), 0)
    col = lax.broadcasted_iota(jnp.int32, (slot_count, quarter), 1)
    wanted = (col // per_owner * 4 + side * 2 + core) * per_owner + col % per_owner
    pick = (row == wanted).astype(BF16)
    own_columns = jnp.dot(router, pick, preferred_element_type=F32).astype(BF16)
    columns = sent_to_all(own_columns, ("xlo", "y")).reshape(width, quarter)

    in_later = kernel_call(
        follow_kernel,
        shape((width, hidden_units), BF16),
        0,
        4 * width * hidden_units,
        [HBM] * 2,
        w_in[0],
        columns,
        scratch=[pltpu.SemaphoreType.DMA((4,))],
        room=16,
    )
    partner_in = lax.ppermute(in_later, "xlo", other())
    out_later = kernel_call(
        follow_kernel,
        shape((hidden_units, width), BF16),
        0,
        4 * width * hidden_units,
        [HBM] * 2,
        w_out[0],
        partner_in,
        scratch=[pltpu.SemaphoreType.DMA((4,))],
        room=16,
    )
    partner_out = lax.ppermute(out_later, "xlo", other())

    message, logits = kernel_call(
        dispatch_kernel,
        (shape((quarter, width + EXTRA), BF16), shape((4 * count, quarter), F32)),
        16 * count * width * quarter,
        2 * (4 * count * width + 2 * width * quarter),
        [HBM] * 7,
        columns,
        *mine,
        *theirs,
        out_specs=(HBM, HBM),
        scratch=[
            pltpu.VMEM((width, quarter), BF16),
            *[pltpu.VMEM(block.shape, BF16) for block in mine + theirs],
            pltpu.VMEM((4 * count, quarter), F32),
            pltpu.VMEM((quarter, width + EXTRA), BF16),
            pltpu.SemaphoreType.DMA((12,)),
        ],
        room=58,
    )
    received = lax.all_to_all(
        message.reshape(owners, per_owner, width + EXTRA), ("xhi", "zh"), 0, 0, tiled=True
    )

    exps, answer = kernel_call(
        exps_kernel,
        (shape((2 * count, quarter + EXTRA), BF16), shape((2 * count, quarter + EXTRA), BF16)),
        64 * count * quarter,
        32 * count * quarter,
        [VMEM],
        logits,
        room=12,
    )
    exps_b = lax.ppermute(answer, "core", other())
    first, second = slice(count, count + middle), slice(count + middle, 2 * count)
    low = lax.ppermute(jnp.concatenate([exps[first], exps_b[first]], axis=1), Z, up)
    high = lax.ppermute(jnp.concatenate([exps[second], exps_b[second]], axis=1), Z, down)
    weights, weights_b = kernel_call(
        weights_kernel,
        (shape((count, 2 * quarter), BF16), shape((count, 2 * quarter), BF16)),
        32 * count * quarter,
        16 * count * quarter,
        [pl.BlockSpec(memory_space=pltpu.SMEM), VMEM, VMEM, VMEM, VMEM],
        jnp.full((1,), side, jnp.int32),
        exps[:count],
        exps_b[:count],
        low,
        high,
        room=12,
    )

    slots = kernel_call(
        pool_kernel,
        shape((groups, per_owner, width), BF16),
        4 * quarter * width,
        2 * quarter * width,
        [VMEM] * 2,
        received,
        norm_gain,
        out_specs=HBM,
        scratch=[pltpu.VMEM((per_owner, width), BF16), pltpu.SemaphoreType.DMA((groups,))],
        room=16,
    )
    rows = lax.all_to_all(slots, "y", 0, 0, tiled=True)
    partial = kernel_call(
        expert_kernel,
        shape((groups, per_owner, width), BF16),
        8 * groups * per_owner * width * hidden_units,
        8 * width * hidden_units,
        [VMEM, HBM, HBM, HBM, HBM, HBM],
        rows,
        w_in[0],
        w_out[0],
        partner_in,
        partner_out,
        exps_b,
        scratch=[
            pltpu.VMEM((width, hidden_units), BF16),
            pltpu.VMEM((hidden_units, width), BF16),
            pltpu.VMEM((width, hidden_units), BF16),
            pltpu.VMEM((hidden_units, width), BF16),
            pltpu.SemaphoreType.DMA((16,)),
        ],
        room=48,
    )
    blocks = lax.all_to_all(partial, "y", 0, 0, tiled=True)
    copies = kernel_call(
        sum_kernel,
        shape((2 * owners, per_owner, width), BF16),
        groups * per_owner * width,
        4 * quarter * width,
        [VMEM, HBM],
        blocks,
        weights,
        out_specs=HBM,
        scratch=[pltpu.VMEM((per_owner, width), BF16), pltpu.SemaphoreType.DMA((2 * owners,))],
        room=16,
    )
    outs = lax.all_to_all(copies, ("zl", "xhi", "zh"), 0, 0, tiled=True).reshape(2 * quarter, width)
    outs_b = lax.ppermute(outs, "core", other())

    mixed = jnp.dot(weights, outs, preferred_element_type=F32)
    mixed += jnp.dot(weights_b, outs_b, preferred_element_type=F32)
    return (feats.astype(F32) + mixed).astype(BF16)[None]


def solution(mesh):
    names = ("xlo", "y", "xhi", "zh", "zl", "core")
    fine = Mesh(mesh.devices.reshape(2, 8, 2, 4, 2, 2), names)
    grp, seq = names[:2], names[2:]
    in_specs = (P(grp, seq, None), P(grp, None), P(seq, None), P(seq, None, grp), P(seq, grp, None))
    return jax.shard_map(
        local, mesh=fine, in_specs=in_specs, out_specs=P(grp, seq, None), check_vma=False
    )
```

```python
import jax
import jax.numpy as jnp
from jax import lax
from jax.experimental import pallas as pl
from jax.experimental.pallas import tpu as pltpu
from jax.sharding import Mesh, PartitionSpec as P

F32 = jnp.float32
BF16 = jnp.bfloat16
EXTRA = 128
Z = ("zh", "zl")
VMEM = pl.BlockSpec(memory_space=pltpu.VMEM)
HBM = pl.BlockSpec(memory_space=pltpu.HBM)


def other(length=2):
    return [(k, k ^ 1) for k in range(length)]


def kernel_call(body, outs, flops, moved, specs, *args, out_specs=None, scratch=(), room=60):
    return pl.pallas_call(
        body,
        out_shape=outs,
        in_specs=specs,
        out_specs=jax.tree.map(lambda _: VMEM, outs) if out_specs is None else out_specs,
        scratch_shapes=scratch,
        compiler_params=pltpu.CompilerParams(vmem_limit_bytes=int(room * 2**20)),
        cost_estimate=pl.CostEstimate(flops=flops, bytes_accessed=moved, transcendentals=0),
    )(*args)


def started(source, target, semaphores, k):
    copy = pltpu.make_async_copy(source, target, semaphores.at[k])
    copy.start()
    return copy


def started_rows(source, target, semaphores, first, count):
    rows = source.shape[0] // count
    parts = [pl.ds(k * rows, rows) for k in range(count)]
    return [started(source.at[p], target.at[p], semaphores, first + k) for k, p in enumerate(parts)]


def split_off(value):
    wide = value * 65537.0
    return wide - (wide - value)


def in_lanes(columns):
    lane = lax.broadcasted_iota(jnp.int32, columns[0].shape, 1)
    packed = jnp.zeros(columns[0].shape, F32)
    for k, column in enumerate(columns):
        first = split_off(column)
        second = split_off(column - first)
        for j, piece in enumerate((first, second, column - first - second)):
            packed = jnp.where(lane == 3 * k + j, piece, packed)
    return packed.astype(BF16)


def dispatch_kernel(*refs):
    sources, refs = refs[:7], refs[7:]
    message_hbm, columns_ref, *feats = refs[:8]
    logits_ref, message_ref, semaphores = refs[8:]
    width, slots = columns_ref.shape
    targets = [columns_ref, *feats]
    loads = [started(source, target, semaphores, k) for k, (source, target) in enumerate(zip(sources, targets))]
    loads[0].wait()
    columns = columns_ref[...]
    offset, high, rows = 0, None, []
    for load, feats_ref in zip(loads[1:], feats):
        load.wait()
        part = slice(offset, offset + feats_ref.shape[0])
        logits = jnp.dot(feats_ref[...], columns, preferred_element_type=F32)
        logits_ref[part, :] = logits
        top = jnp.max(logits, axis=0, keepdims=True)
        high = top if high is None else jnp.maximum(high, top)
        offset += feats_ref.shape[0]
        rows.append(part)
    message_ref[:, width:] = in_lanes([jnp.broadcast_to(high, (EXTRA, slots)).T])
    last = pl.ds(width, EXTRA)
    stores = [started(message_ref.at[:, last], message_hbm.at[:, last], semaphores, 7)]
    dispatch = [jnp.exp(logits_ref[part, :] - high).astype(BF16).T for part in rows]
    step = 512
    for k in range(width // step):
        part = pl.ds(k * step, step)
        sums = jnp.dot(dispatch[0], feats[0][:, part], preferred_element_type=F32)
        for one, feats_ref in zip(dispatch[1:], feats[1:]):
            sums += jnp.dot(one, feats_ref[:, part], preferred_element_type=F32)
        message_ref[:, part] = sums.astype(BF16)
        stores.append(started(message_ref.at[:, part], message_hbm.at[:, part], semaphores, 8 + k))
    for copy in stores:
        copy.wait()


def exps_kernel(columns_ref, *refs):
    feats, (own_ref, answer_ref) = refs[:6], refs[6:]
    columns = columns_ref[...]
    slots = columns.shape[1]
    for k, out_ref in enumerate((own_ref, answer_ref)):
        offset = 0
        for feats_ref in feats[3 * k : 3 * k + 3]:
            rows = feats_ref.shape[0]
            part = slice(offset, offset + rows)
            offset += rows
            logits = jnp.dot(feats_ref[...], columns, preferred_element_type=F32)
            high = jnp.max(logits, axis=1, keepdims=True)
            exps = jnp.exp(logits - high)
            total = jnp.sum(exps, axis=1, keepdims=True)
            out_ref[part, :slots] = exps.astype(BF16)
            lanes = (rows, EXTRA)
            out_ref[part, slots:] = in_lanes([jnp.broadcast_to(high, lanes), jnp.broadcast_to(total, lanes)])


def weights_kernel(side_ref, own_ref, core_ref, low_ref, up_ref, own_weights_ref, core_weights_ref):
    rows, wide = low_ref.shape[0] * 2, own_ref.shape[1]
    slots = wide - EXTRA
    half = rows // 2
    side = side_ref[0]
    for k, given_ref in enumerate((low_ref, up_ref)):
        part = slice(k * half, (k + 1) * half)
        blocks = [own_ref[part, :], core_ref[part, :], given_ref[:, :wide], given_ref[:, wide:]]
        lane = lax.broadcasted_iota(jnp.int32, (half, EXTRA), 1)
        stats = [block[:, slots:].astype(F32) for block in blocks]
        highs = [jnp.sum(jnp.where(lane < 3, s, 0.0), axis=1, keepdims=True) for s in stats]
        sums = [jnp.sum(jnp.where(lane < 3, 0.0, s), axis=1, keepdims=True) for s in stats]
        top = jnp.maximum(jnp.maximum(highs[0], highs[1]), jnp.maximum(highs[2], highs[3]))
        factors = [jnp.exp(high - top) for high in highs]
        total = sums[0] * factors[0] + sums[1] * factors[1] + sums[2] * factors[2] + sums[3] * factors[3]
        scaled = [
            (block[:, :slots].astype(F32) * (factor / total)).astype(BF16)
            for block, factor in zip(blocks, factors)
        ]
        here = pl.ds(pl.multiple_of(side * slots, slots), slots)
        there = pl.ds(pl.multiple_of((1 - side) * slots, slots), slots)
        own_weights_ref[part, here] = scaled[0]
        core_weights_ref[part, here] = scaled[1]
        own_weights_ref[part, there] = scaled[2]
        core_weights_ref[part, there] = scaled[3]


def pool_kernel(received_ref, gain_ref, copies_hbm, slots_ref, semaphores):
    width = gain_ref.shape[1]
    highs = jnp.sum(received_ref[:, :, width:].astype(F32), axis=-1, keepdims=True)
    overall = jnp.max(highs, axis=0, keepdims=True)
    scale = jnp.exp(highs - overall)
    pooled = received_ref[0, :, :width].astype(F32) * scale[0]
    for k in range(1, received_ref.shape[0]):
        pooled += received_ref[k, :, :width].astype(F32) * scale[k]
    mean_sq = jnp.mean(pooled * pooled, axis=-1, keepdims=True)
    slots_ref[...] = (pooled * lax.rsqrt(mean_sq + 1e-06) * gain_ref[...]).astype(BF16)
    copies = [started(slots_ref, copies_hbm.at[k], semaphores, k) for k in range(copies_hbm.shape[0])]
    for copy in copies:
        copy.wait()


def expert_kernel(rows_ref, in_hbm, out_hbm, before_hbm, partial_ref, in_ref, out_ref, semaphores):
    rows = rows_ref[...].reshape(-1, rows_ref.shape[-1])
    width = rows.shape[1]
    loads = [started(in_hbm, in_ref, semaphores, 0), started(out_hbm, out_ref, semaphores, 1)]
    loads[0].wait()
    hidden = jax.nn.gelu(jnp.dot(rows, in_ref[...], preferred_element_type=F32)).astype(BF16)
    loads[1].wait()
    step = 512
    for k in range(width // step):
        part = pl.ds(k * step, step)
        sums = jnp.dot(hidden, out_ref[:, part], preferred_element_type=F32)
        partial_ref[:, :, part] = sums.astype(BF16).reshape(*rows_ref.shape[:2], step)


def sum_kernel(blocks_ref, before_hbm, copies_hbm, total_ref, semaphores):
    total = blocks_ref[0].astype(F32)
    for k in range(1, blocks_ref.shape[0]):
        total += blocks_ref[k].astype(F32)
    total_ref[...] = total.astype(BF16)
    copies = [started(total_ref, copies_hbm.at[k], semaphores, k) for k in range(copies_hbm.shape[0])]
    for copy in copies:
        copy.wait()


def sent_to_all(value, axes):
    length = lax.axis_size(axes)
    return lax.all_to_all(
        jnp.broadcast_to(value[None], (length, *value.shape)), axes, 0, 0, tiled=True
    )


def local(tokens, router, norm_gain, w_in, w_out):
    feats = tokens[0]
    count, width = feats.shape
    slot_count = router.shape[1]
    depth = lax.axis_size(Z)
    owners = lax.axis_size(("xhi", "zh"))
    groups = lax.axis_size(("xlo", "y"))
    per_owner = slot_count // (4 * owners)
    quarter = slot_count // 4
    core, side = lax.axis_index("core"), lax.axis_index("zl")
    hidden_units = w_in.shape[2]
    shape = jax.ShapeDtypeStruct
    up = [(k, (k + 1) % depth) for k in range(depth)]
    down = [(k, (k - 1) % depth) for k in range(depth)]

    middle = count // 2
    above = lax.ppermute(feats[:middle], Z, down)
    below = lax.ppermute(feats[middle:], Z, up)
    mine = [feats, above, below]
    theirs = [lax.ppermute(block, "core", other()) for block in mine]

    row = lax.broadcasted_iota(jnp.int32, (slot_count, quarter), 0)
    col = lax.broadcasted_iota(jnp.int32, (slot_count, quarter), 1)
    wanted = (col // per_owner * 4 + side * 2 + core) * per_owner + col % per_owner
    pick = (row == wanted).astype(BF16)
    own_columns = jnp.dot(router, pick, preferred_element_type=F32).astype(BF16)
    columns = sent_to_all(own_columns, ("xlo", "y")).reshape(width, quarter)

    message = kernel_call(
        dispatch_kernel,
        shape((quarter, width + EXTRA), BF16),
        16 * count * width * quarter,
        2 * (4 * count * width + 2 * width * quarter),
        [HBM] * 7,
        columns,
        *mine,
        *theirs,
        out_specs=HBM,
        scratch=[
            pltpu.VMEM((width, quarter), BF16),
            *[pltpu.VMEM(block.shape, BF16) for block in mine + theirs],
            pltpu.VMEM((4 * count, quarter), F32),
            pltpu.VMEM((quarter, width + EXTRA), BF16),
            pltpu.SemaphoreType.DMA((11,)),
        ],
        room=58,
    )
    received = lax.all_to_all(
        message.reshape(owners, per_owner, width + EXTRA), ("xhi", "zh"), 0, 0, tiled=True
    )

    exps, answer = kernel_call(
        exps_kernel,
        (shape((2 * count, quarter + EXTRA), BF16), shape((2 * count, quarter + EXTRA), BF16)),
        8 * count * width * quarter,
        8 * count * width,
        [VMEM] * 7,
        columns,
        *mine,
        *theirs,
        room=58,
    )
    exps_b = lax.ppermute(answer, "core", other())
    first, second = slice(count, count + middle), slice(count + middle, 2 * count)
    low = lax.ppermute(jnp.concatenate([exps[first], exps_b[first]], axis=1), Z, up)
    high = lax.ppermute(jnp.concatenate([exps[second], exps_b[second]], axis=1), Z, down)
    weights, weights_b = kernel_call(
        weights_kernel,
        (shape((count, 2 * quarter), BF16), shape((count, 2 * quarter), BF16)),
        32 * count * quarter,
        16 * count * quarter,
        [pl.BlockSpec(memory_space=pltpu.SMEM), VMEM, VMEM, VMEM, VMEM],
        jnp.full((1,), side, jnp.int32),
        exps[:count],
        exps_b[:count],
        low,
        high,
        room=12,
    )

    slots = kernel_call(
        pool_kernel,
        shape((groups, per_owner, width), BF16),
        4 * quarter * width,
        2 * quarter * width,
        [VMEM] * 2,
        received,
        norm_gain,
        out_specs=HBM,
        scratch=[pltpu.VMEM((per_owner, width), BF16), pltpu.SemaphoreType.DMA((groups,))],
        room=16,
    )
    rows = lax.all_to_all(slots, ("xlo", "y"), 0, 0, tiled=True)
    partial = kernel_call(
        expert_kernel,
        shape((groups, per_owner, width), BF16),
        4 * groups * per_owner * width * hidden_units,
        4 * width * hidden_units,
        [VMEM, HBM, HBM, HBM],
        rows,
        w_in[0],
        w_out[0],
        exps_b,
        scratch=[
            pltpu.VMEM((width, hidden_units), BF16),
            pltpu.VMEM((hidden_units, width), BF16),
            pltpu.SemaphoreType.DMA((2,)),
        ],
        room=48,
    )
    blocks = lax.all_to_all(partial, ("xlo", "y"), 0, 0, tiled=True)
    copies = kernel_call(
        sum_kernel,
        shape((2 * owners, per_owner, width), BF16),
        groups * per_owner * width,
        4 * quarter * width,
        [VMEM, HBM],
        blocks,
        weights,
        out_specs=HBM,
        scratch=[pltpu.VMEM((per_owner, width), BF16), pltpu.SemaphoreType.DMA((2 * owners,))],
        room=16,
    )
    outs = lax.all_to_all(copies, ("zl", "xhi", "zh"), 0, 0, tiled=True).reshape(2 * quarter, width)
    outs_b = lax.ppermute(outs, "core", other())

    mixed = jnp.dot(weights, outs, preferred_element_type=F32)
    mixed += jnp.dot(weights_b, outs_b, preferred_element_type=F32)
    return (feats.astype(F32) + mixed).astype(BF16)[None]


def solution(mesh):
    names = ("xlo", "y", "xhi", "zh", "zl", "core")
    fine = Mesh(mesh.devices.reshape(2, 8, 2, 4, 2, 2), names)
    grp, seq = names[:2], names[2:]
    in_specs = (P(grp, seq, None), P(grp, None), P(seq, None), P(seq, None, grp), P(seq, grp, None))
    return jax.shard_map(
        local, mesh=fine, in_specs=in_specs, out_specs=P(grp, seq, None), check_vma=False
    )
```

```python
import jax
import jax.numpy as jnp
from jax import lax
from jax.experimental import pallas as pl
from jax.experimental.pallas import tpu as pltpu
from jax.sharding import Mesh, PartitionSpec as P

F32 = jnp.float32
BF16 = jnp.bfloat16
EXTRA = 128
Y = ("yh", "yl")
Z = ("zh", "zl")
VMEM = pl.BlockSpec(memory_space=pltpu.VMEM)
HBM = pl.BlockSpec(memory_space=pltpu.HBM)


def other(length=2):
    return [(k, k ^ 1) for k in range(length)]


def kernel_call(body, outs, flops, moved, specs, *args, out_specs=None, scratch=(), room=60):
    return pl.pallas_call(
        body,
        out_shape=outs,
        in_specs=specs,
        out_specs=jax.tree.map(lambda _: VMEM, outs) if out_specs is None else out_specs,
        scratch_shapes=scratch,
        compiler_params=pltpu.CompilerParams(vmem_limit_bytes=int(room * 2**20)),
        cost_estimate=pl.CostEstimate(flops=flops, bytes_accessed=moved, transcendentals=0),
    )(*args)


def started(source, target, semaphores, k):
    copy = pltpu.make_async_copy(source, target, semaphores.at[k])
    copy.start()
    return copy


def started_rows(source, target, semaphores, first, count):
    rows = source.shape[0] // count
    parts = [pl.ds(k * rows, rows) for k in range(count)]
    return [started(source.at[p], target.at[p], semaphores, first + k) for k, p in enumerate(parts)]


def split_off(value):
    wide = value * 65537.0
    return wide - (wide - value)


def in_lanes(columns):
    lane = lax.broadcasted_iota(jnp.int32, columns[0].shape, 1)
    packed = jnp.zeros(columns[0].shape, F32)
    for k, column in enumerate(columns):
        first = split_off(column)
        second = split_off(column - first)
        for j, piece in enumerate((first, second, column - first - second)):
            packed = jnp.where(lane == 3 * k + j, piece, packed)
    return packed.astype(BF16)


def dispatch_kernel(*refs):
    sources, refs = refs[:7], refs[7:]
    message_hbm, columns_ref, *feats = refs[:8]
    logits_ref, message_ref, semaphores = refs[8:]
    width, slots = columns_ref.shape
    targets = [columns_ref, *feats]
    loads = [started(source, target, semaphores, k) for k, (source, target) in enumerate(zip(sources, targets))]
    loads[0].wait()
    columns = columns_ref[...]
    offset, high, rows = 0, None, []
    for load, feats_ref in zip(loads[1:], feats):
        load.wait()
        part = slice(offset, offset + feats_ref.shape[0])
        logits = jnp.dot(feats_ref[...], columns, preferred_element_type=F32)
        logits_ref[part, :] = logits
        top = jnp.max(logits, axis=0, keepdims=True)
        high = top if high is None else jnp.maximum(high, top)
        offset += feats_ref.shape[0]
        rows.append(part)
    message_ref[:, width:] = in_lanes([jnp.broadcast_to(high, (EXTRA, slots)).T])
    last = pl.ds(width, EXTRA)
    stores = [started(message_ref.at[:, last], message_hbm.at[:, last], semaphores, 7)]
    dispatch = [jnp.exp(logits_ref[part, :] - high).astype(BF16).T for part in rows]
    step = 512
    for k in range(width // step):
        part = pl.ds(k * step, step)
        sums = jnp.dot(dispatch[0], feats[0][:, part], preferred_element_type=F32)
        for one, feats_ref in zip(dispatch[1:], feats[1:]):
            sums += jnp.dot(one, feats_ref[:, part], preferred_element_type=F32)
        message_ref[:, part] = sums.astype(BF16)
        stores.append(started(message_ref.at[:, part], message_hbm.at[:, part], semaphores, 8 + k))
    for copy in stores:
        copy.wait()


def exps_kernel(columns_ref, *refs):
    feats, (own_ref, answer_ref) = refs[:6], refs[6:]
    columns = columns_ref[...]
    slots = columns.shape[1]
    for k, out_ref in enumerate((own_ref, answer_ref)):
        offset = 0
        for feats_ref in feats[3 * k : 3 * k + 3]:
            rows = feats_ref.shape[0]
            part = slice(offset, offset + rows)
            offset += rows
            logits = jnp.dot(feats_ref[...], columns, preferred_element_type=F32)
            high = jnp.max(logits, axis=1, keepdims=True)
            exps = jnp.exp(logits - high)
            total = jnp.sum(exps, axis=1, keepdims=True)
            out_ref[part, :slots] = exps.astype(BF16)
            lanes = (rows, EXTRA)
            out_ref[part, slots:] = in_lanes([jnp.broadcast_to(high, lanes), jnp.broadcast_to(total, lanes)])


def weights_kernel(side_ref, own_ref, core_ref, low_ref, up_ref, own_weights_ref, core_weights_ref):
    rows, wide = low_ref.shape[0] * 2, own_ref.shape[1]
    slots = wide - EXTRA
    half = rows // 2
    side = side_ref[0]
    for k, given_ref in enumerate((low_ref, up_ref)):
        part = slice(k * half, (k + 1) * half)
        blocks = [own_ref[part, :], core_ref[part, :], given_ref[:, :wide], given_ref[:, wide:]]
        lane = lax.broadcasted_iota(jnp.int32, (half, EXTRA), 1)
        stats = [block[:, slots:].astype(F32) for block in blocks]
        highs = [jnp.sum(jnp.where(lane < 3, s, 0.0), axis=1, keepdims=True) for s in stats]
        sums = [jnp.sum(jnp.where(lane < 3, 0.0, s), axis=1, keepdims=True) for s in stats]
        top = jnp.maximum(jnp.maximum(highs[0], highs[1]), jnp.maximum(highs[2], highs[3]))
        factors = [jnp.exp(high - top) for high in highs]
        total = sums[0] * factors[0] + sums[1] * factors[1] + sums[2] * factors[2] + sums[3] * factors[3]
        scaled = [
            (block[:, :slots].astype(F32) * (factor / total)).astype(BF16)
            for block, factor in zip(blocks, factors)
        ]
        here = pl.ds(pl.multiple_of(side * slots, slots), slots)
        there = pl.ds(pl.multiple_of((1 - side) * slots, slots), slots)
        own_weights_ref[part, here] = scaled[0]
        core_weights_ref[part, here] = scaled[1]
        own_weights_ref[part, there] = scaled[2]
        core_weights_ref[part, there] = scaled[3]


def pool_kernel(received_ref, gain_ref, copies_hbm, slots_ref, semaphores):
    width = gain_ref.shape[1]
    highs = jnp.sum(received_ref[:, :, width:].astype(F32), axis=-1, keepdims=True)
    overall = jnp.max(highs, axis=0, keepdims=True)
    scale = jnp.exp(highs - overall)
    pooled = received_ref[0, :, :width].astype(F32) * scale[0]
    for k in range(1, received_ref.shape[0]):
        pooled += received_ref[k, :, :width].astype(F32) * scale[k]
    mean_sq = jnp.mean(pooled * pooled, axis=-1, keepdims=True)
    slots_ref[...] = (pooled * lax.rsqrt(mean_sq + 1e-06) * gain_ref[...]).astype(BF16)
    copies = [started(slots_ref, copies_hbm.at[k], semaphores, k) for k in range(copies_hbm.shape[0])]
    for copy in copies:
        copy.wait()


def expert_kernel(rows_ref, *refs):
    sources, before_hbm, partial_ref, targets, semaphores = refs[:6], refs[6], refs[7], refs[8:14], refs[14]
    rows = rows_ref[...].reshape(-1, rows_ref.shape[-1])
    width = rows.shape[1]
    loads = [started(source, target, semaphores, k) for k, (source, target) in enumerate(zip(sources, targets))]
    hidden = []
    for load, in_ref in zip(loads[:3], targets[:3]):
        load.wait()
        one = jnp.dot(rows, in_ref[...], preferred_element_type=F32)
        hidden.append(jax.nn.gelu(one).astype(BF16))
    for load in loads[3:]:
        load.wait()
    step = 512
    for k in range(width // step):
        part = pl.ds(k * step, step)
        sums = jnp.dot(hidden[0], targets[3][:, part], preferred_element_type=F32)
        sums += jnp.dot(hidden[1], targets[4][:, part], preferred_element_type=F32)
        sums += jnp.dot(hidden[2], targets[5][:, part], preferred_element_type=F32)
        partial_ref[:, :, part] = sums.astype(BF16).reshape(*rows_ref.shape[:2], step)


def sum_kernel(blocks_ref, before_hbm, copies_hbm, total_ref, semaphores):
    total = blocks_ref[0].astype(F32)
    for k in range(1, blocks_ref.shape[0]):
        total += blocks_ref[k].astype(F32)
    total_ref[...] = total.astype(BF16)
    copies = [started(total_ref, copies_hbm.at[k], semaphores, k) for k in range(copies_hbm.shape[0])]
    for copy in copies:
        copy.wait()


def sent_to_all(value, axes):
    length = lax.axis_size(axes)
    return lax.all_to_all(
        jnp.broadcast_to(value[None], (length, *value.shape)), axes, 0, 0, tiled=True
    )


def local(tokens, router, norm_gain, w_in, w_out):
    feats = tokens[0]
    count, width = feats.shape
    slot_count = router.shape[1]
    depth = lax.axis_size(Z)
    owners = lax.axis_size(("xhi", "zh"))
    groups = lax.axis_size(("xlo", "yh"))
    per_owner = slot_count // (4 * owners)
    quarter = slot_count // 4
    core, side = lax.axis_index("core"), lax.axis_index("zl")
    hidden_units = w_in.shape[2]
    shape = jax.ShapeDtypeStruct
    up = [(k, (k + 1) % depth) for k in range(depth)]
    down = [(k, (k - 1) % depth) for k in range(depth)]

    middle = count // 2
    above = lax.ppermute(feats[:middle], Z, down)
    below = lax.ppermute(feats[middle:], Z, up)
    mine = [feats, above, below]
    theirs = [lax.ppermute(block, "core", other()) for block in mine]

    ring = lax.axis_size(Y)
    most = [(2 * k + c, (k + 2 * c - 1) % ring * 2 + c) for k in range(ring) for c in range(2)]
    least = [(2 * k + c, (k + 1 - 2 * c) % ring * 2 + c) for k in range(ring) for c in range(2)]
    cut = hidden_units * 2 // 3
    pairs = [(slice(0, cut), most), (slice(cut, hidden_units), least)]
    given_in = [w_in[0]] + [lax.ppermute(w_in[0, :, part], (*Y, "core"), perm) for part, perm in pairs]
    given_out = [w_out[0]] + [lax.ppermute(w_out[0, part], (*Y, "core"), perm) for part, perm in pairs]

    row = lax.broadcasted_iota(jnp.int32, (slot_count, quarter), 0)
    col = lax.broadcasted_iota(jnp.int32, (slot_count, quarter), 1)
    wanted = (col // per_owner * 4 + side * 2 + core) * per_owner + col % per_owner
    pick = (row == wanted).astype(BF16)
    own_columns = jnp.dot(router, pick, preferred_element_type=F32).astype(BF16)
    columns = sent_to_all(own_columns, ("xlo", *Y)).reshape(width, quarter)

    message = kernel_call(
        dispatch_kernel,
        shape((quarter, width + EXTRA), BF16),
        16 * count * width * quarter,
        2 * (4 * count * width + 2 * width * quarter),
        [HBM] * 7,
        columns,
        *mine,
        *theirs,
        out_specs=HBM,
        scratch=[
            pltpu.VMEM((width, quarter), BF16),
            *[pltpu.VMEM(block.shape, BF16) for block in mine + theirs],
            pltpu.VMEM((4 * count, quarter), F32),
            pltpu.VMEM((quarter, width + EXTRA), BF16),
            pltpu.SemaphoreType.DMA((11,)),
        ],
        room=58,
    )
    received = lax.all_to_all(
        message.reshape(owners, per_owner, width + EXTRA), ("xhi", "zh"), 0, 0, tiled=True
    )

    exps, answer = kernel_call(
        exps_kernel,
        (shape((2 * count, quarter + EXTRA), BF16), shape((2 * count, quarter + EXTRA), BF16)),
        8 * count * width * quarter,
        8 * count * width,
        [VMEM] * 7,
        columns,
        *mine,
        *theirs,
        room=58,
    )
    exps_b = lax.ppermute(answer, "core", other())
    first, second = slice(count, count + middle), slice(count + middle, 2 * count)
    low = lax.ppermute(jnp.concatenate([exps[first], exps_b[first]], axis=1), Z, up)
    high = lax.ppermute(jnp.concatenate([exps[second], exps_b[second]], axis=1), Z, down)
    weights, weights_b = kernel_call(
        weights_kernel,
        (shape((count, 2 * quarter), BF16), shape((count, 2 * quarter), BF16)),
        32 * count * quarter,
        16 * count * quarter,
        [pl.BlockSpec(memory_space=pltpu.SMEM), VMEM, VMEM, VMEM, VMEM],
        jnp.full((1,), side, jnp.int32),
        exps[:count],
        exps_b[:count],
        low,
        high,
        room=12,
    )

    slots = kernel_call(
        pool_kernel,
        shape((groups, per_owner, width), BF16),
        4 * quarter * width,
        2 * quarter * width,
        [VMEM] * 2,
        received,
        norm_gain,
        out_specs=HBM,
        scratch=[pltpu.VMEM((per_owner, width), BF16), pltpu.SemaphoreType.DMA((groups,))],
        room=16,
    )
    rows = lax.all_to_all(slots, ("xlo", "yh"), 0, 0, tiled=True)
    partial = kernel_call(
        expert_kernel,
        shape((groups, per_owner, width), BF16),
        8 * groups * per_owner * width * hidden_units,
        8 * width * hidden_units,
        [VMEM, HBM, HBM, HBM, HBM, HBM, HBM, HBM],
        rows,
        *given_in,
        *given_out,
        exps_b,
        scratch=[
            *[pltpu.VMEM(block.shape, BF16) for block in given_in + given_out],
            pltpu.SemaphoreType.DMA((6,)),
        ],
        room=48,
    )
    blocks = lax.all_to_all(partial, ("xlo", "yh"), 0, 0, tiled=True)
    copies = kernel_call(
        sum_kernel,
        shape((2 * owners, per_owner, width), BF16),
        groups * per_owner * width,
        4 * quarter * width,
        [VMEM, HBM],
        blocks,
        weights,
        out_specs=HBM,
        scratch=[pltpu.VMEM((per_owner, width), BF16), pltpu.SemaphoreType.DMA((2 * owners,))],
        room=16,
    )
    outs = lax.all_to_all(copies, ("zl", "xhi", "zh"), 0, 0, tiled=True).reshape(2 * quarter, width)
    outs_b = lax.ppermute(outs, "core", other())

    mixed = jnp.dot(weights, outs, preferred_element_type=F32)
    mixed += jnp.dot(weights_b, outs_b, preferred_element_type=F32)
    return (feats.astype(F32) + mixed).astype(BF16)[None]


def solution(mesh):
    names = ("xlo", "yh", "yl", "xhi", "zh", "zl", "core")
    fine = Mesh(mesh.devices.reshape(2, 4, 2, 2, 4, 2, 2), names)
    grp, seq = names[:3], names[3:]
    in_specs = (P(grp, seq, None), P(grp, None), P(seq, None), P(seq, None, grp), P(seq, grp, None))
    return jax.shard_map(
        local, mesh=fine, in_specs=in_specs, out_specs=P(grp, seq, None), check_vma=False
    )
```

```python
import jax
import jax.numpy as jnp
from jax import lax
from jax.experimental import pallas as pl
from jax.experimental.pallas import tpu as pltpu
from jax.sharding import Mesh, PartitionSpec as P

F32 = jnp.float32
BF16 = jnp.bfloat16
EXTRA = 128
Y = ("yh", "yl")
Z = ("zh", "zl")
VMEM = pl.BlockSpec(memory_space=pltpu.VMEM)
HBM = pl.BlockSpec(memory_space=pltpu.HBM)


def other(length=2):
    return [(k, k ^ 1) for k in range(length)]


def kernel_call(body, outs, flops, moved, specs, *args, out_specs=None, scratch=(), room=60):
    return pl.pallas_call(
        body,
        out_shape=outs,
        in_specs=specs,
        out_specs=jax.tree.map(lambda _: VMEM, outs) if out_specs is None else out_specs,
        scratch_shapes=scratch,
        compiler_params=pltpu.CompilerParams(vmem_limit_bytes=int(room * 2**20)),
        cost_estimate=pl.CostEstimate(flops=flops, bytes_accessed=moved, transcendentals=0),
    )(*args)


def started(source, target, semaphores, k):
    copy = pltpu.make_async_copy(source, target, semaphores.at[k])
    copy.start()
    return copy


def started_rows(source, target, semaphores, first, count):
    rows = source.shape[0] // count
    parts = [pl.ds(k * rows, rows) for k in range(count)]
    return [started(source.at[p], target.at[p], semaphores, first + k) for k, p in enumerate(parts)]


def split_off(value):
    wide = value * 65537.0
    return wide - (wide - value)


def in_lanes(columns):
    lane = lax.broadcasted_iota(jnp.int32, columns[0].shape, 1)
    packed = jnp.zeros(columns[0].shape, F32)
    for k, column in enumerate(columns):
        first = split_off(column)
        second = split_off(column - first)
        for j, piece in enumerate((first, second, column - first - second)):
            packed = jnp.where(lane == 3 * k + j, piece, packed)
    return packed.astype(BF16)


def dispatch_kernel(*refs):
    sources, refs = refs[:7], refs[7:]
    message_hbm, columns_ref, *feats = refs[:8]
    logits_ref, message_ref, semaphores = refs[8:]
    width, slots = columns_ref.shape
    targets = [columns_ref, *feats]
    loads = [started(source, target, semaphores, k) for k, (source, target) in enumerate(zip(sources, targets))]
    loads[0].wait()
    columns = columns_ref[...]
    offset, high, rows = 0, None, []
    for load, feats_ref in zip(loads[1:], feats):
        load.wait()
        part = slice(offset, offset + feats_ref.shape[0])
        logits = jnp.dot(feats_ref[...], columns, preferred_element_type=F32)
        logits_ref[part, :] = logits
        top = jnp.max(logits, axis=0, keepdims=True)
        high = top if high is None else jnp.maximum(high, top)
        offset += feats_ref.shape[0]
        rows.append(part)
    message_ref[:, width:] = in_lanes([jnp.broadcast_to(high, (EXTRA, slots)).T])
    last = pl.ds(width, EXTRA)
    stores = [started(message_ref.at[:, last], message_hbm.at[:, last], semaphores, 7)]
    dispatch = [jnp.exp(logits_ref[part, :] - high).astype(BF16).T for part in rows]
    step = 512
    for k in range(width // step):
        part = pl.ds(k * step, step)
        sums = jnp.dot(dispatch[0], feats[0][:, part], preferred_element_type=F32)
        for one, feats_ref in zip(dispatch[1:], feats[1:]):
            sums += jnp.dot(one, feats_ref[:, part], preferred_element_type=F32)
        message_ref[:, part] = sums.astype(BF16)
        stores.append(started(message_ref.at[:, part], message_hbm.at[:, part], semaphores, 8 + k))
    for copy in stores:
        copy.wait()


def weights_kernel(side_ref, feats_ref, here_ref, there_ref, here_b_ref, there_b_ref, own_ref, core_ref):
    slots = here_ref.shape[1]
    feats, side = feats_ref[...], side_ref[0]
    columns = (here_ref, there_ref, here_b_ref, there_b_ref)
    logits = [jnp.dot(feats, ref[...], preferred_element_type=F32) for ref in columns]
    tops = [jnp.max(one, axis=1, keepdims=True) for one in logits]
    top = jnp.maximum(jnp.maximum(tops[0], tops[1]), jnp.maximum(tops[2], tops[3]))
    exps = [jnp.exp(one - top) for one in logits]
    sums = [jnp.sum(one, axis=1, keepdims=True) for one in exps]
    scale = 1.0 / (sums[0] + sums[1] + sums[2] + sums[3])
    here = pl.ds(pl.multiple_of(side * slots, slots), slots)
    there = pl.ds(pl.multiple_of((1 - side) * slots, slots), slots)
    for k, (ref, place) in enumerate(((own_ref, here), (own_ref, there), (core_ref, here), (core_ref, there))):
        ref[:, place] = (exps[k] * scale).astype(BF16)


def pool_kernel(received_ref, gain_ref, copies_hbm, slots_ref, semaphores):
    width = gain_ref.shape[1]
    highs = jnp.sum(received_ref[:, :, width:].astype(F32), axis=-1, keepdims=True)
    overall = jnp.max(highs, axis=0, keepdims=True)
    scale = jnp.exp(highs - overall)
    pooled = received_ref[0, :, :width].astype(F32) * scale[0]
    for k in range(1, received_ref.shape[0]):
        pooled += received_ref[k, :, :width].astype(F32) * scale[k]
    mean_sq = jnp.mean(pooled * pooled, axis=-1, keepdims=True)
    slots_ref[...] = (pooled * lax.rsqrt(mean_sq + 1e-06) * gain_ref[...]).astype(BF16)
    copies = [started(slots_ref, copies_hbm.at[k], semaphores, k) for k in range(copies_hbm.shape[0])]
    for copy in copies:
        copy.wait()


def expert_kernel(rows_ref, *refs):
    sources, partial_ref, targets, semaphores = refs[:6], refs[8], refs[9:15], refs[15]
    rows = rows_ref[...].reshape(-1, rows_ref.shape[-1])
    width = rows.shape[1]
    loads = [started(source, target, semaphores, k) for k, (source, target) in enumerate(zip(sources, targets))]
    hidden = []
    for load, in_ref in zip(loads[:3], targets[:3]):
        load.wait()
        one = jnp.dot(rows, in_ref[...], preferred_element_type=F32)
        hidden.append(jax.nn.gelu(one).astype(BF16))
    for load in loads[3:]:
        load.wait()
    step = 512
    for k in range(width // step):
        part = pl.ds(k * step, step)
        sums = jnp.dot(hidden[0], targets[3][:, part], preferred_element_type=F32)
        sums += jnp.dot(hidden[1], targets[4][:, part], preferred_element_type=F32)
        sums += jnp.dot(hidden[2], targets[5][:, part], preferred_element_type=F32)
        partial_ref[:, :, part] = sums.astype(BF16).reshape(*rows_ref.shape[:2], step)


def sum_kernel(blocks_ref, before_hbm, copies_hbm, total_ref, semaphores):
    total = blocks_ref[0].astype(F32)
    for k in range(1, blocks_ref.shape[0]):
        total += blocks_ref[k].astype(F32)
    total_ref[...] = total.astype(BF16)
    copies = [started(total_ref, copies_hbm.at[k], semaphores, k) for k in range(copies_hbm.shape[0])]
    for copy in copies:
        copy.wait()


def sent_to_all(value, axes):
    length = lax.axis_size(axes)
    return lax.all_to_all(
        jnp.broadcast_to(value[None], (length, *value.shape)), axes, 0, 0, tiled=True
    )


def local(tokens, router, norm_gain, w_in, w_out):
    feats = tokens[0]
    count, width = feats.shape
    slot_count = router.shape[1]
    depth = lax.axis_size(Z)
    owners = lax.axis_size(("xhi", "zh"))
    groups = lax.axis_size(("xlo", "yh"))
    per_owner = slot_count // (4 * owners)
    quarter = slot_count // 4
    core, side = lax.axis_index("core"), lax.axis_index("zl")
    hidden_units = w_in.shape[2]
    shape = jax.ShapeDtypeStruct
    up = [(k, (k + 1) % depth) for k in range(depth)]
    down = [(k, (k - 1) % depth) for k in range(depth)]

    middle = count // 2
    above = lax.ppermute(feats[:middle], Z, down)
    below = lax.ppermute(feats[middle:], Z, up)
    mine = [feats, above, below]
    theirs = [lax.ppermute(block, "core", other()) for block in (feats, above, below)]

    ring = lax.axis_size(Y)
    most = [(2 * k + c, (k + 2 * c - 1) % ring * 2 + c) for k in range(ring) for c in range(2)]
    least = [(2 * k + c, (k + 1 - 2 * c) % ring * 2 + c) for k in range(ring) for c in range(2)]
    cut = hidden_units * 2 // 3
    pairs = [(slice(0, cut), most), (slice(cut, hidden_units), least)]
    given_in = [w_in[0]] + [lax.ppermute(w_in[0, :, part], (*Y, "core"), perm) for part, perm in pairs]
    given_out = [w_out[0]] + [lax.ppermute(w_out[0, part], (*Y, "core"), perm) for part, perm in pairs]

    row = lax.broadcasted_iota(jnp.int32, (slot_count, quarter), 0)
    col = lax.broadcasted_iota(jnp.int32, (slot_count, quarter), 1)
    wanted = (col // per_owner * 4 + side * 2 + core) * per_owner + col % per_owner
    pick = (row == wanted).astype(BF16)
    own_columns = jnp.dot(router, pick, preferred_element_type=F32).astype(BF16)
    columns = sent_to_all(own_columns, ("xlo", *Y)).reshape(width, quarter)

    message = kernel_call(
        dispatch_kernel,
        shape((quarter, width + EXTRA), BF16),
        16 * count * width * quarter,
        2 * (4 * count * width + 2 * width * quarter),
        [HBM] * 7,
        columns,
        *mine,
        *theirs,
        out_specs=HBM,
        scratch=[
            pltpu.VMEM((width, quarter), BF16),
            *[pltpu.VMEM(block.shape, BF16) for block in mine + theirs],
            pltpu.VMEM((4 * count, quarter), F32),
            pltpu.VMEM((quarter, width + EXTRA), BF16),
            pltpu.SemaphoreType.DMA((11,)),
        ],
        room=58,
    )
    received = lax.all_to_all(
        message.reshape(owners, per_owner, width + EXTRA), ("xhi", "zh"), 0, 0, tiled=True
    )

    columns_b = lax.ppermute(columns, "core", other())
    far = lax.ppermute(columns, Z, down)
    far_b = lax.ppermute(columns_b, Z, up)
    weights, weights_b = kernel_call(
        weights_kernel,
        (shape((count, 2 * quarter), BF16), shape((count, 2 * quarter), BF16)),
        8 * count * width * quarter,
        2 * count * width + 8 * width * quarter,
        [pl.BlockSpec(memory_space=pltpu.SMEM), *[VMEM] * 5],
        jnp.full((1,), side, jnp.int32),
        feats,
        columns,
        far,
        columns_b,
        far_b,
        room=58,
    )

    slots = kernel_call(
        pool_kernel,
        shape((groups, per_owner, width), BF16),
        4 * quarter * width,
        2 * quarter * width,
        [VMEM] * 2,
        received,
        norm_gain,
        out_specs=HBM,
        scratch=[pltpu.VMEM((per_owner, width), BF16), pltpu.SemaphoreType.DMA((groups,))],
        room=16,
    )
    rows = lax.all_to_all(slots, ("xlo", "yh"), 0, 0, tiled=True)
    partial = kernel_call(
        expert_kernel,
        shape((groups, per_owner, width), BF16),
        8 * groups * per_owner * width * hidden_units,
        8 * width * hidden_units,
        [VMEM, *[HBM] * 8],
        rows,
        *given_in,
        *given_out,
        far,
        far_b,
        scratch=[
            *[pltpu.VMEM(block.shape, BF16) for block in given_in + given_out],
            pltpu.SemaphoreType.DMA((6,)),
        ],
        room=50,
    )
    blocks = lax.all_to_all(partial, ("xlo", "yh"), 0, 0, tiled=True)
    copies = kernel_call(
        sum_kernel,
        shape((2 * owners, per_owner, width), BF16),
        groups * per_owner * width,
        4 * quarter * width,
        [VMEM, HBM],
        blocks,
        weights,
        out_specs=HBM,
        scratch=[pltpu.VMEM((per_owner, width), BF16), pltpu.SemaphoreType.DMA((2 * owners,))],
        room=16,
    )
    outs = lax.all_to_all(copies, ("zl", "xhi", "zh"), 0, 0, tiled=True).reshape(2 * quarter, width)
    outs_b = lax.ppermute(outs, "core", other())

    mixed = jnp.dot(weights, outs, preferred_element_type=F32)
    mixed += jnp.dot(weights_b, outs_b, preferred_element_type=F32)
    return (feats.astype(F32) + mixed).astype(BF16)[None]


def solution(mesh):
    names = ("xlo", "yh", "yl", "xhi", "zh", "zl", "core")
    fine = Mesh(mesh.devices.reshape(2, 4, 2, 2, 4, 2, 2), names)
    grp, seq = names[:3], names[3:]
    in_specs = (P(grp, seq, None), P(grp, None), P(seq, None), P(seq, None, grp), P(seq, grp, None))
    return jax.shard_map(
        local, mesh=fine, in_specs=in_specs, out_specs=P(grp, seq, None), check_vma=False
    )
```

```python
import jax
import jax.numpy as jnp
from jax import lax
from jax.experimental import pallas as pl
from jax.experimental.pallas import tpu as pltpu
from jax.sharding import Mesh, PartitionSpec as P

F32 = jnp.float32
BF16 = jnp.bfloat16
EXTRA = 128
Y = ("yh", "yl")
VMEM = pl.BlockSpec(memory_space=pltpu.VMEM)
HBM = pl.BlockSpec(memory_space=pltpu.HBM)


def other(length=2):
    return [(k, k ^ 1) for k in range(length)]


def kernel_call(body, outs, flops, moved, specs, *args, out_specs=None, scratch=(), room=60):
    return pl.pallas_call(
        body,
        out_shape=outs,
        in_specs=specs,
        out_specs=jax.tree.map(lambda _: VMEM, outs) if out_specs is None else out_specs,
        scratch_shapes=scratch,
        compiler_params=pltpu.CompilerParams(vmem_limit_bytes=int(room * 2**20)),
        cost_estimate=pl.CostEstimate(flops=flops, bytes_accessed=moved, transcendentals=0),
    )(*args)


def started(source, target, semaphores, k):
    copy = pltpu.make_async_copy(source, target, semaphores.at[k])
    copy.start()
    return copy


def started_rows(source, target, semaphores, first, count):
    rows = source.shape[0] // count
    parts = [pl.ds(k * rows, rows) for k in range(count)]
    return [started(source.at[p], target.at[p], semaphores, first + k) for k, p in enumerate(parts)]


def split_off(value):
    wide = value * 65537.0
    return wide - (wide - value)


def in_lanes(columns):
    lane = lax.broadcasted_iota(jnp.int32, columns[0].shape, 1)
    packed = jnp.zeros(columns[0].shape, F32)
    for k, column in enumerate(columns):
        first = split_off(column)
        second = split_off(column - first)
        for j, piece in enumerate((first, second, column - first - second)):
            packed = jnp.where(lane == 3 * k + j, piece, packed)
    return packed.astype(BF16)


def dispatch_kernel(
    columns_hbm, own_hbm, partner_hbm, message_hbm, columns_ref, own_ref, partner_ref, message_ref, semaphores
):
    width, slots = columns_ref.shape
    loads = [
        started(columns_hbm, columns_ref, semaphores, 0),
        started(own_hbm, own_ref, semaphores, 1),
        started(partner_hbm, partner_ref, semaphores, 2),
    ]
    loads[0].wait()
    columns = columns_ref[...]
    loads[1].wait()
    own_logits = jnp.dot(own_ref[...], columns, preferred_element_type=F32)
    loads[2].wait()
    partner_logits = jnp.dot(partner_ref[...], columns, preferred_element_type=F32)
    high = jnp.maximum(
        jnp.max(own_logits, axis=0, keepdims=True), jnp.max(partner_logits, axis=0, keepdims=True)
    )
    message_ref[:, width:] = in_lanes([jnp.broadcast_to(high, (EXTRA, slots)).T])
    last = pl.ds(width, EXTRA)
    stores = [started(message_ref.at[:, last], message_hbm.at[:, last], semaphores, 3)]
    own = jnp.exp(own_logits - high).astype(BF16).T
    partner = jnp.exp(partner_logits - high).astype(BF16).T
    step = 384
    for k in range(width // step):
        part = pl.ds(k * step, step)
        sums = jnp.dot(own, own_ref[:, part], preferred_element_type=F32)
        sums += jnp.dot(partner, partner_ref[:, part], preferred_element_type=F32)
        message_ref[:, part] = sums.astype(BF16)
        stores.append(started(message_ref.at[:, part], message_hbm.at[:, part], semaphores, 4 + k))
    for copy in stores:
        copy.wait()


def softmax_kernel(columns_ref, own_feats_ref, partner_feats_ref, own_ref, answer_ref):
    columns = columns_ref[...]
    for feats_ref, out_ref in ((own_feats_ref, own_ref), (partner_feats_ref, answer_ref)):
        logits = jnp.dot(feats_ref[...], columns, preferred_element_type=F32)
        slots = logits.shape[1]
        high = jnp.max(logits, axis=1, keepdims=True)
        exps = jnp.exp(logits - high)
        total = jnp.sum(exps, axis=1, keepdims=True)
        out_ref[:, :slots] = exps.astype(BF16)
        lanes = (logits.shape[0], EXTRA)
        out_ref[:, slots:] = in_lanes([jnp.broadcast_to(high, lanes), jnp.broadcast_to(total, lanes)])


def pool_kernel(received_ref, gain_ref, copies_hbm, slots_ref, semaphores):
    width = gain_ref.shape[1]
    highs = jnp.sum(received_ref[:, :, width:].astype(F32), axis=-1, keepdims=True)
    overall = jnp.max(highs, axis=0, keepdims=True)
    scale = jnp.exp(highs - overall)
    pooled = received_ref[0, :, :width].astype(F32) * scale[0]
    for k in range(1, received_ref.shape[0]):
        pooled += received_ref[k, :, :width].astype(F32) * scale[k]
    mean_sq = jnp.mean(pooled * pooled, axis=-1, keepdims=True)
    slots_ref[...] = (pooled * lax.rsqrt(mean_sq + 1e-06) * gain_ref[...]).astype(BF16)
    copies = [started(slots_ref, copies_hbm.at[k], semaphores, k) for k in range(copies_hbm.shape[0])]
    for copy in copies:
        copy.wait()


def expert_kernel(rows_ref, *refs):
    sources, partial_ref, targets, semaphores = refs[:6], refs[6], refs[7:13], refs[13]
    rows = rows_ref[...].reshape(-1, rows_ref.shape[-1])
    width = rows.shape[1]
    loads = [started(source, target, semaphores, k) for k, (source, target) in enumerate(zip(sources, targets))]
    hidden = []
    for load, in_ref in zip(loads[:3], targets[:3]):
        load.wait()
        one = jnp.dot(rows, in_ref[...], preferred_element_type=F32)
        hidden.append(jax.nn.gelu(one).astype(BF16))
    for load in loads[3:]:
        load.wait()
    step = 512
    for k in range(width // step):
        part = pl.ds(k * step, step)
        sums = jnp.dot(hidden[0], targets[3][:, part], preferred_element_type=F32)
        sums += jnp.dot(hidden[1], targets[4][:, part], preferred_element_type=F32)
        sums += jnp.dot(hidden[2], targets[5][:, part], preferred_element_type=F32)
        partial_ref[:, :, part] = sums.astype(BF16).reshape(*rows_ref.shape[:2], step)


def sum_kernel(blocks_ref, copies_hbm, total_ref, semaphores):
    total = blocks_ref[0].astype(F32)
    for k in range(1, blocks_ref.shape[0]):
        total += blocks_ref[k].astype(F32)
    total_ref[...] = total.astype(BF16)
    copies = [started(total_ref, copies_hbm.at[k], semaphores, k) for k in range(copies_hbm.shape[0])]
    for copy in copies:
        copy.wait()


def piece_sum(block, which):
    part = block[:, 3 * which : 3 * which + 3].astype(F32)
    return part[:, 0] + part[:, 1] + part[:, 2]


def sent_to_all(value, axes):
    length = lax.axis_size(axes)
    return lax.all_to_all(
        jnp.broadcast_to(value[None], (length, *value.shape)), axes, 0, 0, tiled=True
    )


def local(tokens, router, norm_gain, w_in, w_out):
    feats = tokens[0]
    count, width = feats.shape
    slot_count = router.shape[1]
    owners = lax.axis_size(("xhi", "z"))
    groups = lax.axis_size(("xlo", "yh"))
    per_owner = slot_count // (2 * owners)
    half = slot_count // 2
    core = lax.axis_index("core")
    hidden_units = w_in.shape[2]
    shape = jax.ShapeDtypeStruct

    partner_feats = lax.ppermute(feats, "core", other())

    ring = lax.axis_size(Y)
    most = [(2 * k + c, (k + 2 * c - 1) % ring * 2 + c) for k in range(ring) for c in range(2)]
    least = [(2 * k + c, (k + 1 - 2 * c) % ring * 2 + c) for k in range(ring) for c in range(2)]
    cut = hidden_units * 2 // 3
    pairs = [(slice(0, cut), most), (slice(cut, hidden_units), least)]
    given_in = [w_in[0]] + [lax.ppermute(w_in[0, :, part], (*Y, "core"), perm) for part, perm in pairs]
    given_out = [w_out[0]] + [lax.ppermute(w_out[0, part], (*Y, "core"), perm) for part, perm in pairs]

    row = lax.broadcasted_iota(jnp.int32, (slot_count, half), 0)
    col = lax.broadcasted_iota(jnp.int32, (slot_count, half), 1)
    wanted = (col // per_owner * 2 + core) * per_owner + col % per_owner
    pick = (row == wanted).astype(BF16)
    own_columns = jnp.dot(router, pick, preferred_element_type=F32).astype(BF16)
    columns = sent_to_all(own_columns, ("xlo", *Y)).reshape(width, half)

    message = kernel_call(
        dispatch_kernel,
        shape((half, width + EXTRA), BF16),
        8 * count * width * half,
        2 * (2 * count * width + 2 * width * half),
        [HBM] * 3,
        columns,
        feats,
        partner_feats,
        out_specs=HBM,
        scratch=[
            pltpu.VMEM((width, half), BF16),
            pltpu.VMEM((count, width), BF16),
            pltpu.VMEM((count, width), BF16),
            pltpu.VMEM((half, width + EXTRA), BF16),
            pltpu.SemaphoreType.DMA((8,)),
        ],
        room=50,
    )
    received = lax.all_to_all(
        message.reshape(owners, per_owner, width + EXTRA), ("xhi", "z"), 0, 0, tiled=True
    )

    weights, answer = kernel_call(
        softmax_kernel,
        (shape((count, half + EXTRA), BF16), shape((count, half + EXTRA), BF16)),
        4 * count * width * half,
        4 * count * width,
        [VMEM] * 3,
        columns,
        feats,
        partner_feats,
        room=58,
    )
    weights_b = lax.ppermute(answer, "core", other())

    slots = kernel_call(
        pool_kernel,
        shape((groups, per_owner, width), BF16),
        4 * half * width,
        2 * half * width,
        [VMEM] * 2,
        received,
        norm_gain,
        out_specs=HBM,
        scratch=[pltpu.VMEM((per_owner, width), BF16), pltpu.SemaphoreType.DMA((groups,))],
        room=16,
    )
    rows = lax.all_to_all(slots, ("xlo", "yh"), 0, 0, tiled=True)
    partial = kernel_call(
        expert_kernel,
        shape((groups, per_owner, width), BF16),
        8 * groups * per_owner * width * hidden_units,
        8 * width * hidden_units,
        [VMEM, *[HBM] * 6],
        rows,
        *given_in,
        *given_out,
        scratch=[
            *[pltpu.VMEM(block.shape, BF16) for block in given_in + given_out],
            pltpu.SemaphoreType.DMA((6,)),
        ],
        room=50,
    )
    blocks = lax.all_to_all(partial, ("xlo", "yh"), 0, 0, tiled=True)
    copies = kernel_call(
        sum_kernel,
        shape((owners, per_owner, width), BF16),
        groups * per_owner * width,
        2 * half * width,
        [VMEM],
        blocks,
        out_specs=HBM,
        scratch=[pltpu.VMEM((per_owner, width), BF16), pltpu.SemaphoreType.DMA((owners,))],
        room=16,
    )
    outs = lax.all_to_all(copies, ("xhi", "z"), 0, 0, tiled=True).reshape(half, width)
    outs_b = lax.ppermute(outs, "core", other())

    stats, stats_b = weights[:, half:], weights_b[:, half:]
    row_high, row_sum = piece_sum(stats, 0), piece_sum(stats, 1)
    row_high_b, row_sum_b = piece_sum(stats_b, 0), piece_sum(stats_b, 1)
    top = jnp.maximum(row_high, row_high_b)
    factor = jnp.exp(row_high - top)
    factor_b = jnp.exp(row_high_b - top)
    total = row_sum * factor + row_sum_b * factor_b
    mixed = jnp.dot(weights[:, :half], outs, preferred_element_type=F32) * (factor / total)[:, None]
    mixed += jnp.dot(weights_b[:, :half], outs_b, preferred_element_type=F32) * (factor_b / total)[:, None]
    return (feats.astype(F32) + mixed).astype(BF16)[None]


def solution(mesh):
    fine = Mesh(mesh.devices.reshape(2, 4, 2, 2, 8, 2), ("xlo", "yh", "yl", "xhi", "z", "core"))
    grp, seq = ("xlo", *Y), ("xhi", "z", "core")
    in_specs = (P(grp, seq, None), P(grp, None), P(seq, None), P(seq, None, grp), P(seq, grp, None))
    return jax.shard_map(
        local, mesh=fine, in_specs=in_specs, out_specs=P(grp, seq, None), check_vma=False
    )
```

```python
import functools

import jax
import jax.numpy as jnp
from jax import lax
from jax.experimental import pallas as pl
from jax.experimental.pallas import tpu as pltpu
from jax.sharding import Mesh, PartitionSpec as P

F32 = jnp.float32
BF16 = jnp.bfloat16
EXTRA = 128
Y = ("yh", "yl")
VMEM = pl.BlockSpec(memory_space=pltpu.VMEM)
HBM = pl.BlockSpec(memory_space=pltpu.HBM)


def other(length=2):
    return [(k, k ^ 1) for k in range(length)]


def kernel_call(body, outs, flops, moved, specs, *args, out_specs=None, scratch=(), room=60):
    return pl.pallas_call(
        body,
        out_shape=outs,
        in_specs=specs,
        out_specs=jax.tree.map(lambda _: VMEM, outs) if out_specs is None else out_specs,
        scratch_shapes=scratch,
        compiler_params=pltpu.CompilerParams(vmem_limit_bytes=int(room * 2**20)),
        cost_estimate=pl.CostEstimate(flops=flops, bytes_accessed=moved, transcendentals=0),
    )(*args)


def started(source, target, semaphores, k):
    copy = pltpu.make_async_copy(source, target, semaphores.at[k])
    copy.start()
    return copy


def started_rows(source, target, semaphores, first, count):
    rows = source.shape[0] // count
    parts = [pl.ds(k * rows, rows) for k in range(count)]
    return [started(source.at[p], target.at[p], semaphores, first + k) for k, p in enumerate(parts)]


def split_off(value):
    wide = value * 65537.0
    return wide - (wide - value)


def in_lanes(columns):
    lane = lax.broadcasted_iota(jnp.int32, columns[0].shape, 1)
    packed = jnp.zeros(columns[0].shape, F32)
    for k, column in enumerate(columns):
        first = split_off(column)
        second = split_off(column - first)
        for j, piece in enumerate((first, second, column - first - second)):
            packed = jnp.where(lane == 3 * k + j, piece, packed)
    return packed.astype(BF16)


def dispatch_kernel(
    columns_hbm, own_hbm, partner_hbm, message_hbm, columns_ref, own_ref, partner_ref, message_ref, semaphores
):
    width, slots = columns_ref.shape
    loads = [
        started(columns_hbm, columns_ref, semaphores, 0),
        started(own_hbm, own_ref, semaphores, 1),
        started(partner_hbm, partner_ref, semaphores, 2),
    ]
    loads[0].wait()
    columns = columns_ref[...]
    loads[1].wait()
    own_logits = jnp.dot(own_ref[...], columns, preferred_element_type=F32)
    loads[2].wait()
    partner_logits = jnp.dot(partner_ref[...], columns, preferred_element_type=F32)
    high = jnp.maximum(
        jnp.max(own_logits, axis=0, keepdims=True), jnp.max(partner_logits, axis=0, keepdims=True)
    )
    message_ref[:, width:] = in_lanes([jnp.broadcast_to(high, (EXTRA, slots)).T])
    last = pl.ds(width, EXTRA)
    stores = [started(message_ref.at[:, last], message_hbm.at[:, last], semaphores, 3)]
    own = jnp.exp(own_logits - high).astype(BF16).T
    partner = jnp.exp(partner_logits - high).astype(BF16).T
    step = 384
    for k in range(width // step):
        part = pl.ds(k * step, step)
        sums = jnp.dot(own, own_ref[:, part], preferred_element_type=F32)
        sums += jnp.dot(partner, partner_ref[:, part], preferred_element_type=F32)
        message_ref[:, part] = sums.astype(BF16)
        stores.append(started(message_ref.at[:, part], message_hbm.at[:, part], semaphores, 4 + k))
    for copy in stores:
        copy.wait()


def softmax_kernel(columns_ref, own_feats_ref, partner_feats_ref, own_ref, answer_ref):
    columns = columns_ref[...]
    for feats_ref, out_ref in ((own_feats_ref, own_ref), (partner_feats_ref, answer_ref)):
        logits = jnp.dot(feats_ref[...], columns, preferred_element_type=F32)
        slots = logits.shape[1]
        high = jnp.max(logits, axis=1, keepdims=True)
        exps = jnp.exp(logits - high)
        total = jnp.sum(exps, axis=1, keepdims=True)
        out_ref[:, :slots] = exps.astype(BF16)
        lanes = (logits.shape[0], EXTRA)
        out_ref[:, slots:] = in_lanes([jnp.broadcast_to(high, lanes), jnp.broadcast_to(total, lanes)])


def pool_kernel(received_ref, gain_ref, copies_hbm, slots_ref, semaphores):
    width = gain_ref.shape[1]
    highs = jnp.sum(received_ref[:, :, width:].astype(F32), axis=-1, keepdims=True)
    overall = jnp.max(highs, axis=0, keepdims=True)
    scale = jnp.exp(highs - overall)
    pooled = received_ref[0, :, :width].astype(F32) * scale[0]
    for k in range(1, received_ref.shape[0]):
        pooled += received_ref[k, :, :width].astype(F32) * scale[k]
    mean_sq = jnp.mean(pooled * pooled, axis=-1, keepdims=True)
    slots_ref[...] = (pooled * lax.rsqrt(mean_sq + 1e-06) * gain_ref[...]).astype(BF16)
    copies = [started(slots_ref, copies_hbm.at[k], semaphores, k) for k in range(copies_hbm.shape[0])]
    for copy in copies:
        copy.wait()


def pack_kernel(first, count, in_hbm, out_hbm, before_hbm, packed_ref, semaphores):
    width = in_hbm.shape[0]
    copies = [started(in_hbm.at[:, pl.ds(first, count)], packed_ref.at[pl.ds(0, width)], semaphores, 0)]
    for k in range(width // count):
        block = out_hbm.at[pl.ds(first, count), pl.ds(k * count, count)]
        copies.append(started(block, packed_ref.at[pl.ds(width + k * count, count)], semaphores, 1 + k))
    for copy in copies:
        copy.wait()


def expert_kernel(rows_ref, *refs):
    sources, partial_ref, targets, semaphores = refs[:4], refs[4], refs[5:9], refs[9]
    rows = rows_ref[...].reshape(-1, rows_ref.shape[-1])
    width = rows.shape[1]
    loads = [started(source, target, semaphores, k) for k, (source, target) in enumerate(zip(sources, targets))]
    in_ref, *packed, out_ref = targets
    hidden = []
    for load, ref in zip(loads, (in_ref, *packed)):
        load.wait()
        one = jnp.dot(rows, ref[:width, :], preferred_element_type=F32)
        hidden.append(jax.nn.gelu(one).astype(BF16))
    loads[3].wait()
    step = 512
    for start in range(0, width, step):
        sums = jnp.dot(hidden[0], out_ref[:, start : start + step], preferred_element_type=F32)
        for one, ref in zip(hidden[1:], packed):
            count = ref.shape[1]
            blocks = [
                jnp.dot(one, ref[width + k : width + k + count, :], preferred_element_type=F32)
                for k in range(start, start + step, count)
            ]
            sums += jnp.concatenate(blocks, axis=1)
        partial_ref[:, :, start : start + step] = sums.astype(BF16).reshape(*rows_ref.shape[:2], step)


def scale_kernel(own_ref, core_ref, own_weights_ref, core_weights_ref):
    slots = own_weights_ref.shape[1]
    blocks = (own_ref, core_ref)
    stats = [ref[:, slots:].astype(F32) for ref in blocks]
    lane = lax.broadcasted_iota(jnp.int32, stats[0].shape, 1)
    highs = [jnp.sum(jnp.where(lane < 3, one, 0.0), axis=1, keepdims=True) for one in stats]
    sums = [jnp.sum(jnp.where(lane < 3, 0.0, one), axis=1, keepdims=True) for one in stats]
    top = jnp.maximum(highs[0], highs[1])
    factors = [jnp.exp(high - top) for high in highs]
    total = sums[0] * factors[0] + sums[1] * factors[1]
    for ref, out_ref, factor in zip(blocks, (own_weights_ref, core_weights_ref), factors):
        out_ref[...] = (ref[:, :slots].astype(F32) * (factor / total)).astype(BF16)


def sum_kernel(blocks_ref, before_hbm, copies_hbm, total_ref, semaphores):
    total = blocks_ref[0].astype(F32)
    for k in range(1, blocks_ref.shape[0]):
        total += blocks_ref[k].astype(F32)
    total_ref[...] = total.astype(BF16)
    copies = [started(total_ref, copies_hbm.at[k], semaphores, k) for k in range(copies_hbm.shape[0])]
    for copy in copies:
        copy.wait()


def sent_to_all(value, axes):
    length = lax.axis_size(axes)
    return lax.all_to_all(
        jnp.broadcast_to(value[None], (length, *value.shape)), axes, 0, 0, tiled=True
    )


def local(tokens, router, norm_gain, w_in, w_out):
    feats = tokens[0]
    count, width = feats.shape
    slot_count = router.shape[1]
    owners = lax.axis_size(("xhi", "z"))
    groups = lax.axis_size(("xlo", "yh"))
    per_owner = slot_count // (2 * owners)
    half = slot_count // 2
    core = lax.axis_index("core")
    hidden_units = w_in.shape[2]
    shape = jax.ShapeDtypeStruct

    partner_feats = lax.ppermute(feats, "core", other())

    ring = lax.axis_size(Y)
    most = [(2 * k + c, (k + 2 * c - 1) % ring * 2 + c) for k in range(ring) for c in range(2)]
    least = [(2 * k + c, (k + 1 - 2 * c) % ring * 2 + c) for k in range(ring) for c in range(2)]
    cut = hidden_units * 2 // 3
    given = []
    for first, units, perm in ((0, cut, most), (cut, hidden_units - cut, least)):
        packed = kernel_call(
            functools.partial(pack_kernel, first, units),
            shape((2 * width, units), BF16),
            0,
            8 * width * units,
            [HBM] * 3,
            w_in[0],
            w_out[0],
            given[0] if given else router,
            scratch=[pltpu.SemaphoreType.DMA((1 + width // units,))],
            room=16,
        )
        given.append(lax.ppermute(packed, (*Y, "core"), perm))

    row = lax.broadcasted_iota(jnp.int32, (slot_count, half), 0)
    col = lax.broadcasted_iota(jnp.int32, (slot_count, half), 1)
    wanted = (col // per_owner * 2 + core) * per_owner + col % per_owner
    pick = (row == wanted).astype(BF16)
    own_columns = jnp.dot(router, pick, preferred_element_type=F32).astype(BF16)
    columns = sent_to_all(own_columns, ("xlo", *Y)).reshape(width, half)

    message = kernel_call(
        dispatch_kernel,
        shape((half, width + EXTRA), BF16),
        8 * count * width * half,
        2 * (2 * count * width + 2 * width * half),
        [HBM] * 3,
        columns,
        feats,
        partner_feats,
        out_specs=HBM,
        scratch=[
            pltpu.VMEM((width, half), BF16),
            pltpu.VMEM((count, width), BF16),
            pltpu.VMEM((count, width), BF16),
            pltpu.VMEM((half, width + EXTRA), BF16),
            pltpu.SemaphoreType.DMA((8,)),
        ],
        room=56,
    )
    received = lax.all_to_all(
        message.reshape(owners, per_owner, width + EXTRA), ("xhi", "z"), 0, 0, tiled=True
    )

    exps, answer = kernel_call(
        softmax_kernel,
        (shape((count, half + EXTRA), BF16), shape((count, half + EXTRA), BF16)),
        4 * count * width * half,
        4 * count * width,
        [VMEM] * 3,
        columns,
        feats,
        partner_feats,
        room=58,
    )
    answer = lax.ppermute(answer, "core", other())
    weights, weights_b = kernel_call(
        scale_kernel,
        (shape((count, half), BF16), shape((count, half), BF16)),
        8 * count * half,
        8 * count * half,
        [VMEM] * 2,
        exps,
        answer,
        room=16,
    )

    slots = kernel_call(
        pool_kernel,
        shape((groups, per_owner, width), BF16),
        4 * half * width,
        2 * half * width,
        [VMEM] * 2,
        received,
        norm_gain,
        out_specs=HBM,
        scratch=[pltpu.VMEM((per_owner, width), BF16), pltpu.SemaphoreType.DMA((groups,))],
        room=16,
    )
    rows = lax.all_to_all(slots, ("xlo", "yh"), 0, 0, tiled=True)
    partial = kernel_call(
        expert_kernel,
        shape((groups, per_owner, width), BF16),
        8 * groups * per_owner * width * hidden_units,
        8 * width * hidden_units,
        [VMEM, *[HBM] * 4],
        rows,
        w_in[0],
        *given,
        w_out[0],
        scratch=[
            pltpu.VMEM((width, hidden_units), BF16),
            *[pltpu.VMEM(block.shape, BF16) for block in given],
            pltpu.VMEM((hidden_units, width), BF16),
            pltpu.SemaphoreType.DMA((4,)),
        ],
        room=50,
    )
    blocks = lax.all_to_all(partial, ("xlo", "yh"), 0, 0, tiled=True)
    copies = kernel_call(
        sum_kernel,
        shape((owners, per_owner, width), BF16),
        groups * per_owner * width,
        2 * half * width,
        [VMEM, HBM],
        blocks,
        weights,
        out_specs=HBM,
        scratch=[pltpu.VMEM((per_owner, width), BF16), pltpu.SemaphoreType.DMA((owners,))],
        room=16,
    )
    outs = lax.all_to_all(copies, ("xhi", "z"), 0, 0, tiled=True).reshape(half, width)
    outs_b = lax.ppermute(outs, "core", other())

    mixed = jnp.dot(weights, outs, preferred_element_type=F32)
    mixed += jnp.dot(weights_b, outs_b, preferred_element_type=F32)
    return (feats.astype(F32) + mixed).astype(BF16)[None]


def solution(mesh):
    fine = Mesh(mesh.devices.reshape(2, 4, 2, 2, 8, 2), ("xlo", "yh", "yl", "xhi", "z", "core"))
    grp, seq = ("xlo", *Y), ("xhi", "z", "core")
    in_specs = (P(grp, seq, None), P(grp, None), P(seq, None), P(seq, None, grp), P(seq, grp, None))
    return jax.shard_map(
        local, mesh=fine, in_specs=in_specs, out_specs=P(grp, seq, None), check_vma=False
    )
```

```python
import functools

import jax
import jax.numpy as jnp
from jax import lax
from jax.experimental import pallas as pl
from jax.experimental.pallas import tpu as pltpu
from jax.sharding import Mesh, PartitionSpec as P

F32 = jnp.float32
BF16 = jnp.bfloat16
EXTRA = 128
Y = ("yh", "yl")
VMEM = pl.BlockSpec(memory_space=pltpu.VMEM)
HBM = pl.BlockSpec(memory_space=pltpu.HBM)


def other(length=2):
    return [(k, k ^ 1) for k in range(length)]


def kernel_call(body, outs, flops, moved, specs, *args, out_specs=None, scratch=(), room=60):
    return pl.pallas_call(
        body,
        out_shape=outs,
        in_specs=specs,
        out_specs=jax.tree.map(lambda _: VMEM, outs) if out_specs is None else out_specs,
        scratch_shapes=scratch,
        compiler_params=pltpu.CompilerParams(vmem_limit_bytes=int(room * 2**20)),
        cost_estimate=pl.CostEstimate(flops=flops, bytes_accessed=moved, transcendentals=0),
    )(*args)


def started(source, target, semaphores, k):
    copy = pltpu.make_async_copy(source, target, semaphores.at[k])
    copy.start()
    return copy


def started_rows(source, target, semaphores, first, count):
    rows = source.shape[0] // count
    parts = [pl.ds(k * rows, rows) for k in range(count)]
    return [started(source.at[p], target.at[p], semaphores, first + k) for k, p in enumerate(parts)]


def split_off(value):
    wide = value * 65537.0
    return wide - (wide - value)


def in_lanes(columns):
    lane = lax.broadcasted_iota(jnp.int32, columns[0].shape, 1)
    packed = jnp.zeros(columns[0].shape, F32)
    for k, column in enumerate(columns):
        first = split_off(column)
        second = split_off(column - first)
        for j, piece in enumerate((first, second, column - first - second)):
            packed = jnp.where(lane == 3 * k + j, piece, packed)
    return packed.astype(BF16)


def dispatch_kernel(
    columns_hbm, own_hbm, partner_hbm, message_hbm, columns_ref, own_ref, partner_ref, message_ref, semaphores
):
    width, slots = columns_ref.shape
    loads = [
        started(columns_hbm, columns_ref, semaphores, 0),
        started(own_hbm, own_ref, semaphores, 1),
        started(partner_hbm, partner_ref, semaphores, 2),
    ]
    loads[0].wait()
    columns = columns_ref[...]
    loads[1].wait()
    own_logits = jnp.dot(own_ref[...], columns, preferred_element_type=F32)
    loads[2].wait()
    partner_logits = jnp.dot(partner_ref[...], columns, preferred_element_type=F32)
    high = jnp.maximum(
        jnp.max(own_logits, axis=0, keepdims=True), jnp.max(partner_logits, axis=0, keepdims=True)
    )
    message_ref[:, width:] = in_lanes([jnp.broadcast_to(high, (EXTRA, slots)).T])
    last = pl.ds(width, EXTRA)
    stores = [started(message_ref.at[:, last], message_hbm.at[:, last], semaphores, 3)]
    own = jnp.exp(own_logits - high).astype(BF16).T
    partner = jnp.exp(partner_logits - high).astype(BF16).T
    step = 384
    for k in range(width // step):
        part = pl.ds(k * step, step)
        sums = jnp.dot(own, own_ref[:, part], preferred_element_type=F32)
        sums += jnp.dot(partner, partner_ref[:, part], preferred_element_type=F32)
        message_ref[:, part] = sums.astype(BF16)
        stores.append(started(message_ref.at[:, part], message_hbm.at[:, part], semaphores, 4 + k))
    for copy in stores:
        copy.wait()


def softmax_kernel(columns_ref, own_feats_ref, partner_feats_ref, own_ref, answer_ref):
    columns = columns_ref[...]
    for feats_ref, out_ref in ((own_feats_ref, own_ref), (partner_feats_ref, answer_ref)):
        logits = jnp.dot(feats_ref[...], columns, preferred_element_type=F32)
        slots = logits.shape[1]
        high = jnp.max(logits, axis=1, keepdims=True)
        exps = jnp.exp(logits - high)
        total = jnp.sum(exps, axis=1, keepdims=True)
        out_ref[:, :slots] = exps.astype(BF16)
        lanes = (logits.shape[0], EXTRA)
        out_ref[:, slots:] = in_lanes([jnp.broadcast_to(high, lanes), jnp.broadcast_to(total, lanes)])


def pool_kernel(received_ref, gain_ref, copies_hbm, slots_ref, semaphores):
    width = gain_ref.shape[1]
    highs = jnp.sum(received_ref[:, :, width:].astype(F32), axis=-1, keepdims=True)
    overall = jnp.max(highs, axis=0, keepdims=True)
    scale = jnp.exp(highs - overall)
    pooled = received_ref[0, :, :width].astype(F32) * scale[0]
    for k in range(1, received_ref.shape[0]):
        pooled += received_ref[k, :, :width].astype(F32) * scale[k]
    mean_sq = jnp.mean(pooled * pooled, axis=-1, keepdims=True)
    slots_ref[...] = (pooled * lax.rsqrt(mean_sq + 1e-06) * gain_ref[...]).astype(BF16)
    copies = [started(slots_ref, copies_hbm.at[k], semaphores, k) for k in range(copies_hbm.shape[0])]
    for copy in copies:
        copy.wait()


def pack_kernel(first, count, in_hbm, out_hbm, before_hbm, packed_ref, semaphores):
    width = in_hbm.shape[0]
    copies = [started(in_hbm.at[:, pl.ds(first, count)], packed_ref.at[pl.ds(0, width)], semaphores, 0)]
    for k in range(width // count):
        block = out_hbm.at[pl.ds(first, count), pl.ds(k * count, count)]
        copies.append(started(block, packed_ref.at[pl.ds(width + k * count, count)], semaphores, 1 + k))
    for copy in copies:
        copy.wait()


def expert_kernel(rows_ref, *refs):
    sources, partial_ref, targets, semaphores = refs[:4], refs[4], refs[5:9], refs[9]
    rows = rows_ref[...].reshape(-1, rows_ref.shape[-1])
    width = rows.shape[1]
    loads = [started(source, target, semaphores, k) for k, (source, target) in enumerate(zip(sources, targets))]
    in_ref, *packed, out_ref = targets
    hidden = []
    for load, ref in zip(loads, (in_ref, *packed)):
        load.wait()
        one = jnp.dot(rows, ref[:width, :], preferred_element_type=F32)
        hidden.append(jax.nn.gelu(one).astype(BF16))
    loads[3].wait()
    step = 512
    for start in range(0, width, step):
        sums = jnp.dot(hidden[0], out_ref[:, start : start + step], preferred_element_type=F32)
        for one, ref in zip(hidden[1:], packed):
            count = ref.shape[1]
            blocks = [
                jnp.dot(one, ref[width + k : width + k + count, :], preferred_element_type=F32)
                for k in range(start, start + step, count)
            ]
            sums += jnp.concatenate(blocks, axis=1)
        partial_ref[:, :, start : start + step] = sums.astype(BF16).reshape(*rows_ref.shape[:2], step)


def scale_kernel(own_ref, core_ref, own_weights_ref, core_weights_ref):
    slots = own_weights_ref.shape[1]
    blocks = (own_ref, core_ref)
    stats = [ref[:, slots:].astype(F32) for ref in blocks]
    lane = lax.broadcasted_iota(jnp.int32, stats[0].shape, 1)
    highs = [jnp.sum(jnp.where(lane < 3, one, 0.0), axis=1, keepdims=True) for one in stats]
    sums = [jnp.sum(jnp.where(lane < 3, 0.0, one), axis=1, keepdims=True) for one in stats]
    top = jnp.maximum(highs[0], highs[1])
    factors = [jnp.exp(high - top) for high in highs]
    total = sums[0] * factors[0] + sums[1] * factors[1]
    for ref, out_ref, factor in zip(blocks, (own_weights_ref, core_weights_ref), factors):
        out_ref[...] = (ref[:, :slots].astype(F32) * (factor / total)).astype(BF16)


def sum_kernel(blocks_ref, before_hbm, copies_hbm, total_ref, semaphores):
    total = blocks_ref[0].astype(F32)
    for k in range(1, blocks_ref.shape[0]):
        total += blocks_ref[k].astype(F32)
    total_ref[...] = total.astype(BF16)
    copies = [started(total_ref, copies_hbm.at[k], semaphores, k) for k in range(copies_hbm.shape[0])]
    for copy in copies:
        copy.wait()


def sent_to_all(value, axes):
    length = lax.axis_size(axes)
    return lax.all_to_all(
        jnp.broadcast_to(value[None], (length, *value.shape)), axes, 0, 0, tiled=True
    )


def local(tokens, router, norm_gain, w_in, w_out):
    feats = tokens[0]
    count, width = feats.shape
    slot_count = router.shape[1]
    owners = lax.axis_size(("xhi", "z"))
    groups = lax.axis_size(("xlo", "yh"))
    per_owner = slot_count // (2 * owners)
    half = slot_count // 2
    core = lax.axis_index("core")
    hidden_units = w_in.shape[2]
    shape = jax.ShapeDtypeStruct

    partner_feats = lax.ppermute(feats, "core", other())

    ring = lax.axis_size(Y)
    most = [(2 * k + c, (k + 2 * c - 1) % ring * 2 + c) for k in range(ring) for c in range(2)]
    least = [(2 * k + c, (k + 1 - 2 * c) % ring * 2 + c) for k in range(ring) for c in range(2)]
    cut = hidden_units * 2 // 3
    given = []
    for first, units, perm in ((0, cut, most), (cut, hidden_units - cut, least)):
        packed = kernel_call(
            functools.partial(pack_kernel, first, units),
            shape((2 * width, units), BF16),
            0,
            8 * width * units,
            [HBM] * 3,
            w_in[0],
            w_out[0],
            given[0] if given else router,
            scratch=[pltpu.SemaphoreType.DMA((1 + width // units,))],
            room=16,
        )
        given.append(lax.ppermute(packed, (*Y, "core"), perm))

    row = lax.broadcasted_iota(jnp.int32, (slot_count, half), 0)
    col = lax.broadcasted_iota(jnp.int32, (slot_count, half), 1)
    wanted = (col // per_owner * 2 + core) * per_owner + col % per_owner
    pick = (row == wanted).astype(BF16)
    own_columns = jnp.dot(router, pick, preferred_element_type=F32).astype(BF16)
    columns = sent_to_all(own_columns, ("xlo", *Y)).reshape(width, half)

    message = kernel_call(
        dispatch_kernel,
        shape((half, width + EXTRA), BF16),
        8 * count * width * half,
        2 * (2 * count * width + 2 * width * half),
        [HBM] * 3,
        columns,
        feats,
        partner_feats,
        out_specs=HBM,
        scratch=[
            pltpu.VMEM((width, half), BF16),
            pltpu.VMEM((count, width), BF16),
            pltpu.VMEM((count, width), BF16),
            pltpu.VMEM((half, width + EXTRA), BF16),
            pltpu.SemaphoreType.DMA((8,)),
        ],
        room=56,
    )
    received = lax.all_to_all(
        message.reshape(owners, per_owner, width + EXTRA), ("xhi", "z"), 0, 0, tiled=True
    )

    exps, answer = kernel_call(
        softmax_kernel,
        (shape((count, half + EXTRA), BF16), shape((count, half + EXTRA), BF16)),
        4 * count * width * half,
        4 * count * width,
        [VMEM] * 3,
        columns,
        feats,
        partner_feats,
        room=58,
    )
    answer = lax.ppermute(answer, "core", other())
    weights, weights_b = kernel_call(
        scale_kernel,
        (shape((count, half), BF16), shape((count, half), BF16)),
        8 * count * half,
        8 * count * half,
        [VMEM] * 2,
        exps,
        answer,
        room=16,
    )

    slots = kernel_call(
        pool_kernel,
        shape((groups, per_owner, width), BF16),
        4 * half * width,
        2 * half * width,
        [VMEM] * 2,
        received,
        norm_gain,
        out_specs=HBM,
        scratch=[pltpu.VMEM((per_owner, width), BF16), pltpu.SemaphoreType.DMA((groups,))],
        room=16,
    )
    rows = lax.all_to_all(slots, ("xlo", "yh"), 0, 0, tiled=True)
    partial = kernel_call(
        expert_kernel,
        shape((groups, per_owner, width), BF16),
        8 * groups * per_owner * width * hidden_units,
        8 * width * hidden_units,
        [VMEM, *[HBM] * 4],
        rows,
        w_in[0],
        *given,
        w_out[0],
        scratch=[
            pltpu.VMEM((width, hidden_units), BF16),
            *[pltpu.VMEM(block.shape, BF16) for block in given],
            pltpu.VMEM((hidden_units, width), BF16),
            pltpu.SemaphoreType.DMA((4,)),
        ],
        room=50,
    )
    blocks = lax.all_to_all(partial, ("xlo", "yh"), 0, 0, tiled=True)
    copies = kernel_call(
        sum_kernel,
        shape((owners, per_owner, width), BF16),
        groups * per_owner * width,
        2 * half * width,
        [VMEM, HBM],
        blocks,
        weights,
        out_specs=HBM,
        scratch=[pltpu.VMEM((per_owner, width), BF16), pltpu.SemaphoreType.DMA((owners,))],
        room=16,
    )
    outs = lax.all_to_all(copies, ("xhi", "z"), 0, 0, tiled=True).reshape(half, width)
    outs_b = lax.ppermute(outs, "core", other())

    near = feats.astype(F32) + jnp.dot(weights, outs, preferred_element_type=F32)
    near = lax.optimization_barrier(near)
    far = jnp.dot(weights_b, outs_b, preferred_element_type=F32)
    return (near + far).astype(BF16)[None]


def solution(mesh):
    fine = Mesh(mesh.devices.reshape(2, 4, 2, 2, 8, 2), ("xlo", "yh", "yl", "xhi", "z", "core"))
    grp, seq = ("xlo", *Y), ("xhi", "z", "core")
    in_specs = (P(grp, seq, None), P(grp, None), P(seq, None), P(seq, None, grp), P(seq, grp, None))
    return jax.shard_map(
        local, mesh=fine, in_specs=in_specs, out_specs=P(grp, seq, None), check_vma=False
    )
```

```python
import functools

import jax
import jax.numpy as jnp
from jax import lax
from jax.experimental import pallas as pl
from jax.experimental.pallas import tpu as pltpu
from jax.sharding import Mesh, PartitionSpec as P

F32 = jnp.float32
BF16 = jnp.bfloat16
EXTRA = 128
Y = ("yh", "yl")
VMEM = pl.BlockSpec(memory_space=pltpu.VMEM)
HBM = pl.BlockSpec(memory_space=pltpu.HBM)


def other(length=2):
    return [(k, k ^ 1) for k in range(length)]


def kernel_call(body, outs, flops, moved, specs, *args, out_specs=None, scratch=(), room=60):
    return pl.pallas_call(
        body,
        out_shape=outs,
        in_specs=specs,
        out_specs=jax.tree.map(lambda _: VMEM, outs) if out_specs is None else out_specs,
        scratch_shapes=scratch,
        compiler_params=pltpu.CompilerParams(vmem_limit_bytes=int(room * 2**20)),
        cost_estimate=pl.CostEstimate(flops=flops, bytes_accessed=moved, transcendentals=0),
    )(*args)


def started(source, target, semaphores, k):
    copy = pltpu.make_async_copy(source, target, semaphores.at[k])
    copy.start()
    return copy


def started_rows(source, target, semaphores, first, count):
    rows = source.shape[0] // count
    parts = [pl.ds(k * rows, rows) for k in range(count)]
    return [started(source.at[p], target.at[p], semaphores, first + k) for k, p in enumerate(parts)]


def split_off(value):
    wide = value * 65537.0
    return wide - (wide - value)


def in_lanes(columns):
    lane = lax.broadcasted_iota(jnp.int32, columns[0].shape, 1)
    packed = jnp.zeros(columns[0].shape, F32)
    for k, column in enumerate(columns):
        first = split_off(column)
        second = split_off(column - first)
        for j, piece in enumerate((first, second, column - first - second)):
            packed = jnp.where(lane == 3 * k + j, piece, packed)
    return packed.astype(BF16)


def columns_kernel(per_owner, core_ref, router_ref, copies_hbm, own_ref, semaphores):
    half = own_ref.shape[1]
    shape = (router_ref.shape[1], half)
    row = lax.broadcasted_iota(jnp.int32, shape, 0)
    col = lax.broadcasted_iota(jnp.int32, shape, 1)
    wanted = (col // per_owner * 2 + core_ref[0]) * per_owner + col % per_owner
    pick = jnp.where(row == wanted, 1.0, 0.0).astype(BF16)
    own_ref[...] = jnp.dot(router_ref[...], pick, preferred_element_type=F32).astype(BF16)
    copies = [started(own_ref, copies_hbm.at[k], semaphores, k) for k in range(copies_hbm.shape[0])]
    for copy in copies:
        copy.wait()


def dispatch_kernel(
    columns_hbm, own_hbm, partner_hbm, message_hbm, columns_ref, own_ref, partner_ref, message_ref, semaphores
):
    width, slots = columns_ref.shape
    loads = [
        started(columns_hbm, columns_ref, semaphores, 0),
        started(own_hbm, own_ref, semaphores, 1),
        started(partner_hbm, partner_ref, semaphores, 2),
    ]
    loads[0].wait()
    columns = columns_ref[...]
    loads[1].wait()
    own_logits = jnp.dot(own_ref[...], columns, preferred_element_type=F32)
    loads[2].wait()
    partner_logits = jnp.dot(partner_ref[...], columns, preferred_element_type=F32)
    high = jnp.maximum(
        jnp.max(own_logits, axis=0, keepdims=True), jnp.max(partner_logits, axis=0, keepdims=True)
    )
    message_ref[:, width:] = in_lanes([jnp.broadcast_to(high, (EXTRA, slots)).T])
    last = pl.ds(width, EXTRA)
    stores = [started(message_ref.at[:, last], message_hbm.at[:, last], semaphores, 3)]
    own = jnp.exp(own_logits - high).astype(BF16).T
    partner = jnp.exp(partner_logits - high).astype(BF16).T
    step = 384
    for k in range(width // step):
        part = pl.ds(k * step, step)
        sums = jnp.dot(own, own_ref[:, part], preferred_element_type=F32)
        sums += jnp.dot(partner, partner_ref[:, part], preferred_element_type=F32)
        message_ref[:, part] = sums.astype(BF16)
        stores.append(started(message_ref.at[:, part], message_hbm.at[:, part], semaphores, 4 + k))
    for copy in stores:
        copy.wait()


def softmax_kernel(columns_ref, own_feats_ref, partner_feats_ref, own_ref, answer_ref):
    columns = columns_ref[...]
    for feats_ref, out_ref in ((own_feats_ref, own_ref), (partner_feats_ref, answer_ref)):
        logits = jnp.dot(feats_ref[...], columns, preferred_element_type=F32)
        slots = logits.shape[1]
        high = jnp.max(logits, axis=1, keepdims=True)
        exps = jnp.exp(logits - high)
        total = jnp.sum(exps, axis=1, keepdims=True)
        out_ref[:, :slots] = exps.astype(BF16)
        lanes = (logits.shape[0], EXTRA)
        out_ref[:, slots:] = in_lanes([jnp.broadcast_to(high, lanes), jnp.broadcast_to(total, lanes)])


def pool_kernel(received_ref, gain_ref, copies_hbm, slots_ref, semaphores):
    width = gain_ref.shape[1]
    highs = jnp.sum(received_ref[:, :, width:].astype(F32), axis=-1, keepdims=True)
    overall = jnp.max(highs, axis=0, keepdims=True)
    scale = jnp.exp(highs - overall)
    pooled = received_ref[0, :, :width].astype(F32) * scale[0]
    for k in range(1, received_ref.shape[0]):
        pooled += received_ref[k, :, :width].astype(F32) * scale[k]
    mean_sq = jnp.mean(pooled * pooled, axis=-1, keepdims=True)
    slots_ref[...] = (pooled * lax.rsqrt(mean_sq + 1e-06) * gain_ref[...]).astype(BF16)
    copies = [started(slots_ref, copies_hbm.at[k], semaphores, k) for k in range(copies_hbm.shape[0])]
    for copy in copies:
        copy.wait()


def pack_kernel(first, count, in_hbm, out_hbm, before_hbm, packed_ref, semaphores):
    width = in_hbm.shape[0]
    copies = [started(in_hbm.at[:, pl.ds(first, count)], packed_ref.at[pl.ds(0, width)], semaphores, 0)]
    for k in range(width // count):
        block = out_hbm.at[pl.ds(first, count), pl.ds(k * count, count)]
        copies.append(started(block, packed_ref.at[pl.ds(width + k * count, count)], semaphores, 1 + k))
    for copy in copies:
        copy.wait()


def expert_kernel(rows_ref, *refs):
    sources, partial_ref, targets, semaphores = refs[:4], refs[4], refs[5:9], refs[9]
    rows = rows_ref[...].reshape(-1, rows_ref.shape[-1])
    width = rows.shape[1]
    loads = [started(source, target, semaphores, k) for k, (source, target) in enumerate(zip(sources, targets))]
    in_ref, *packed, out_ref = targets
    hidden = []
    for load, ref in zip(loads, (in_ref, *packed)):
        load.wait()
        one = jnp.dot(rows, ref[:width, :], preferred_element_type=F32)
        hidden.append(jax.nn.gelu(one).astype(BF16))
    loads[3].wait()
    step = 512
    for start in range(0, width, step):
        sums = jnp.dot(hidden[0], out_ref[:, start : start + step], preferred_element_type=F32)
        for one, ref in zip(hidden[1:], packed):
            count = ref.shape[1]
            blocks = [
                jnp.dot(one, ref[width + k : width + k + count, :], preferred_element_type=F32)
                for k in range(start, start + step, count)
            ]
            sums += jnp.concatenate(blocks, axis=1)
        partial_ref[:, :, start : start + step] = sums.astype(BF16).reshape(*rows_ref.shape[:2], step)


def scale_kernel(own_ref, core_ref, own_weights_ref, core_weights_ref):
    slots = own_weights_ref.shape[1]
    blocks = (own_ref, core_ref)
    stats = [ref[:, slots:].astype(F32) for ref in blocks]
    lane = lax.broadcasted_iota(jnp.int32, stats[0].shape, 1)
    highs = [jnp.sum(jnp.where(lane < 3, one, 0.0), axis=1, keepdims=True) for one in stats]
    sums = [jnp.sum(jnp.where(lane < 3, 0.0, one), axis=1, keepdims=True) for one in stats]
    top = jnp.maximum(highs[0], highs[1])
    factors = [jnp.exp(high - top) for high in highs]
    total = sums[0] * factors[0] + sums[1] * factors[1]
    for ref, out_ref, factor in zip(blocks, (own_weights_ref, core_weights_ref), factors):
        out_ref[...] = (ref[:, :slots].astype(F32) * (factor / total)).astype(BF16)


def sum_kernel(blocks_ref, before_hbm, copies_hbm, total_ref, semaphores):
    total = blocks_ref[0].astype(F32)
    for k in range(1, blocks_ref.shape[0]):
        total += blocks_ref[k].astype(F32)
    total_ref[...] = total.astype(BF16)
    copies = [started(total_ref, copies_hbm.at[k], semaphores, k) for k in range(copies_hbm.shape[0])]
    for copy in copies:
        copy.wait()


def local(tokens, router, norm_gain, w_in, w_out):
    feats = tokens[0]
    count, width = feats.shape
    slot_count = router.shape[1]
    owners = lax.axis_size(("xhi", "z"))
    groups = lax.axis_size(("xlo", "yh"))
    per_owner = slot_count // (2 * owners)
    half = slot_count // 2
    core = lax.axis_index("core")
    hidden_units = w_in.shape[2]
    shape = jax.ShapeDtypeStruct

    partner_feats = lax.ppermute(feats, "core", other())

    ring = lax.axis_size(Y)
    most = [(2 * k + c, (k + 2 * c - 1) % ring * 2 + c) for k in range(ring) for c in range(2)]
    least = [(2 * k + c, (k + 1 - 2 * c) % ring * 2 + c) for k in range(ring) for c in range(2)]
    cut = hidden_units * 2 // 3
    given = []
    for first, units, perm in ((0, cut, most), (cut, hidden_units - cut, least)):
        packed = kernel_call(
            functools.partial(pack_kernel, first, units),
            shape((2 * width, units), BF16),
            0,
            8 * width * units,
            [HBM] * 3,
            w_in[0],
            w_out[0],
            given[0] if given else router,
            scratch=[pltpu.SemaphoreType.DMA((1 + width // units,))],
            room=16,
        )
        given.append(lax.ppermute(packed, (*Y, "core"), perm))

    copies = kernel_call(
        functools.partial(columns_kernel, per_owner),
        shape((2 * groups, router.shape[0], half), BF16),
        2 * router.shape[0] * slot_count * half,
        4 * width * half,
        [pl.BlockSpec(memory_space=pltpu.SMEM), VMEM],
        jnp.full((1,), core, jnp.int32),
        router,
        out_specs=HBM,
        scratch=[pltpu.VMEM((router.shape[0], half), BF16), pltpu.SemaphoreType.DMA((2 * groups,))],
        room=58,
    )
    columns = lax.all_to_all(copies, ("xlo", *Y), 0, 0, tiled=True).reshape(width, half)

    message = kernel_call(
        dispatch_kernel,
        shape((half, width + EXTRA), BF16),
        8 * count * width * half,
        2 * (2 * count * width + 2 * width * half),
        [HBM] * 3,
        columns,
        feats,
        partner_feats,
        out_specs=HBM,
        scratch=[
            pltpu.VMEM((width, half), BF16),
            pltpu.VMEM((count, width), BF16),
            pltpu.VMEM((count, width), BF16),
            pltpu.VMEM((half, width + EXTRA), BF16),
            pltpu.SemaphoreType.DMA((8,)),
        ],
        room=56,
    )
    received = lax.all_to_all(
        message.reshape(owners, per_owner, width + EXTRA), ("xhi", "z"), 0, 0, tiled=True
    )

    exps, answer = kernel_call(
        softmax_kernel,
        (shape((count, half + EXTRA), BF16), shape((count, half + EXTRA), BF16)),
        4 * count * width * half,
        4 * count * width,
        [VMEM] * 3,
        columns,
        feats,
        partner_feats,
        room=58,
    )
    answer = lax.ppermute(answer, "core", other())
    weights, weights_b = kernel_call(
        scale_kernel,
        (shape((count, half), BF16), shape((count, half), BF16)),
        8 * count * half,
        8 * count * half,
        [VMEM] * 2,
        exps,
        answer,
        room=16,
    )

    slots = kernel_call(
        pool_kernel,
        shape((groups, per_owner, width), BF16),
        4 * half * width,
        2 * half * width,
        [VMEM] * 2,
        received,
        norm_gain,
        out_specs=HBM,
        scratch=[pltpu.VMEM((per_owner, width), BF16), pltpu.SemaphoreType.DMA((groups,))],
        room=16,
    )
    rows = lax.all_to_all(slots, ("xlo", "yh"), 0, 0, tiled=True)
    partial = kernel_call(
        expert_kernel,
        shape((groups, per_owner, width), BF16),
        8 * groups * per_owner * width * hidden_units,
        8 * width * hidden_units,
        [VMEM, *[HBM] * 4],
        rows,
        w_in[0],
        *given,
        w_out[0],
        scratch=[
            pltpu.VMEM((width, hidden_units), BF16),
            *[pltpu.VMEM(block.shape, BF16) for block in given],
            pltpu.VMEM((hidden_units, width), BF16),
            pltpu.SemaphoreType.DMA((4,)),
        ],
        room=50,
    )
    blocks = lax.all_to_all(partial, ("xlo", "yh"), 0, 0, tiled=True)
    copies = kernel_call(
        sum_kernel,
        shape((owners, per_owner, width), BF16),
        groups * per_owner * width,
        2 * half * width,
        [VMEM, HBM],
        blocks,
        weights,
        out_specs=HBM,
        scratch=[pltpu.VMEM((per_owner, width), BF16), pltpu.SemaphoreType.DMA((owners,))],
        room=16,
    )
    outs = lax.all_to_all(copies, ("xhi", "z"), 0, 0, tiled=True).reshape(half, width)
    outs_b = lax.ppermute(outs, "core", other())

    near = feats.astype(F32) + jnp.dot(weights, outs, preferred_element_type=F32)
    near = lax.optimization_barrier(near)
    far = jnp.dot(weights_b, outs_b, preferred_element_type=F32)
    return (near + far).astype(BF16)[None]


def solution(mesh):
    fine = Mesh(mesh.devices.reshape(2, 4, 2, 2, 8, 2), ("xlo", "yh", "yl", "xhi", "z", "core"))
    grp, seq = ("xlo", *Y), ("xhi", "z", "core")
    in_specs = (P(grp, seq, None), P(grp, None), P(seq, None), P(seq, None, grp), P(seq, grp, None))
    return jax.shard_map(
        local, mesh=fine, in_specs=in_specs, out_specs=P(grp, seq, None), check_vma=False
    )
```

```python
import functools

import jax
import jax.numpy as jnp
from jax import lax
from jax.experimental import pallas as pl
from jax.experimental.pallas import tpu as pltpu
from jax.sharding import Mesh, PartitionSpec as P

F32 = jnp.float32
BF16 = jnp.bfloat16
EXTRA = 128
Y = ("yh", "yl")
VMEM = pl.BlockSpec(memory_space=pltpu.VMEM)
HBM = pl.BlockSpec(memory_space=pltpu.HBM)


def other(length=2):
    return [(k, k ^ 1) for k in range(length)]


def kernel_call(body, outs, flops, moved, specs, *args, out_specs=None, scratch=(), room=60):
    return pl.pallas_call(
        body,
        out_shape=outs,
        in_specs=specs,
        out_specs=jax.tree.map(lambda _: VMEM, outs) if out_specs is None else out_specs,
        scratch_shapes=scratch,
        compiler_params=pltpu.CompilerParams(vmem_limit_bytes=int(room * 2**20)),
        cost_estimate=pl.CostEstimate(flops=flops, bytes_accessed=moved, transcendentals=0),
    )(*args)


def started(source, target, semaphores, k):
    copy = pltpu.make_async_copy(source, target, semaphores.at[k])
    copy.start()
    return copy


def started_rows(source, target, semaphores, first, count):
    rows = source.shape[0] // count
    parts = [pl.ds(k * rows, rows) for k in range(count)]
    return [started(source.at[p], target.at[p], semaphores, first + k) for k, p in enumerate(parts)]


def split_off(value):
    wide = value * 65537.0
    return wide - (wide - value)


def in_lanes(columns):
    lane = lax.broadcasted_iota(jnp.int32, columns[0].shape, 1)
    packed = jnp.zeros(columns[0].shape, F32)
    for k, column in enumerate(columns):
        first = split_off(column)
        second = split_off(column - first)
        for j, piece in enumerate((first, second, column - first - second)):
            packed = jnp.where(lane == 3 * k + j, piece, packed)
    return packed.astype(BF16)


def columns_kernel(per_owner, core_ref, router_ref, copies_hbm, own_ref, semaphores):
    half = own_ref.shape[1]
    shape = (router_ref.shape[1], half)
    row = lax.broadcasted_iota(jnp.int32, shape, 0)
    col = lax.broadcasted_iota(jnp.int32, shape, 1)
    bits = per_owner.bit_length() - 1
    wanted = ((((col >> bits) << 1) + core_ref[0]) << bits) + (col & (per_owner - 1))
    pick = jnp.where(row == wanted, 1.0, 0.0).astype(BF16)
    own_ref[...] = jnp.dot(router_ref[...], pick, preferred_element_type=F32).astype(BF16)
    copies = [started(own_ref, copies_hbm.at[k], semaphores, k) for k in range(copies_hbm.shape[0])]
    for copy in copies:
        copy.wait()


def dispatch_kernel(
    columns_hbm, own_hbm, partner_hbm, message_hbm, columns_ref, own_ref, partner_ref, message_ref, semaphores
):
    width, slots = columns_ref.shape
    loads = [
        started(columns_hbm, columns_ref, semaphores, 0),
        started(own_hbm, own_ref, semaphores, 1),
        started(partner_hbm, partner_ref, semaphores, 2),
    ]
    loads[0].wait()
    columns = columns_ref[...]
    loads[1].wait()
    own_logits = jnp.dot(own_ref[...], columns, preferred_element_type=F32)
    loads[2].wait()
    partner_logits = jnp.dot(partner_ref[...], columns, preferred_element_type=F32)
    high = jnp.maximum(
        jnp.max(own_logits, axis=0, keepdims=True), jnp.max(partner_logits, axis=0, keepdims=True)
    )
    message_ref[:, width:] = in_lanes([jnp.broadcast_to(high, (EXTRA, slots)).T])
    last = pl.ds(width, EXTRA)
    stores = [started(message_ref.at[:, last], message_hbm.at[:, last], semaphores, 3)]
    own = jnp.exp(own_logits - high).astype(BF16).T
    partner = jnp.exp(partner_logits - high).astype(BF16).T
    step = 384
    for k in range(width // step):
        part = pl.ds(k * step, step)
        sums = jnp.dot(own, own_ref[:, part], preferred_element_type=F32)
        sums += jnp.dot(partner, partner_ref[:, part], preferred_element_type=F32)
        message_ref[:, part] = sums.astype(BF16)
        stores.append(started(message_ref.at[:, part], message_hbm.at[:, part], semaphores, 4 + k))
    for copy in stores:
        copy.wait()


def softmax_kernel(columns_ref, own_feats_ref, partner_feats_ref, own_ref, answer_ref):
    columns = columns_ref[...]
    for feats_ref, out_ref in ((own_feats_ref, own_ref), (partner_feats_ref, answer_ref)):
        logits = jnp.dot(feats_ref[...], columns, preferred_element_type=F32)
        slots = logits.shape[1]
        high = jnp.max(logits, axis=1, keepdims=True)
        exps = jnp.exp(logits - high)
        total = jnp.sum(exps, axis=1, keepdims=True)
        out_ref[:, :slots] = exps.astype(BF16)
        lanes = (logits.shape[0], EXTRA)
        out_ref[:, slots:] = in_lanes([jnp.broadcast_to(high, lanes), jnp.broadcast_to(total, lanes)])


def pool_kernel(received_ref, gain_ref, copies_hbm, slots_ref, semaphores):
    width = gain_ref.shape[1]
    highs = jnp.sum(received_ref[:, :, width:].astype(F32), axis=-1, keepdims=True)
    overall = jnp.max(highs, axis=0, keepdims=True)
    scale = jnp.exp(highs - overall)
    pooled = received_ref[0, :, :width].astype(F32) * scale[0]
    for k in range(1, received_ref.shape[0]):
        pooled += received_ref[k, :, :width].astype(F32) * scale[k]
    mean_sq = jnp.mean(pooled * pooled, axis=-1, keepdims=True)
    slots_ref[...] = (pooled * lax.rsqrt(mean_sq + 1e-06) * gain_ref[...]).astype(BF16)
    copies = [started(slots_ref, copies_hbm.at[k], semaphores, k) for k in range(copies_hbm.shape[0])]
    for copy in copies:
        copy.wait()


def pack_kernel(first, count, in_hbm, out_hbm, before_hbm, packed_ref, semaphores):
    width = in_hbm.shape[0]
    copies = [started(in_hbm.at[:, pl.ds(first, count)], packed_ref.at[pl.ds(0, width)], semaphores, 0)]
    for k in range(width // count):
        block = out_hbm.at[pl.ds(first, count), pl.ds(k * count, count)]
        copies.append(started(block, packed_ref.at[pl.ds(width + k * count, count)], semaphores, 1 + k))
    for copy in copies:
        copy.wait()


def expert_kernel(rows_ref, *refs):
    sources, partial_ref, targets, semaphores = refs[:4], refs[4], refs[5:9], refs[9]
    rows = rows_ref[...].reshape(-1, rows_ref.shape[-1])
    width = rows.shape[1]
    loads = [started(source, target, semaphores, k) for k, (source, target) in enumerate(zip(sources, targets))]
    in_ref, *packed, out_ref = targets
    hidden = []
    for load, ref in zip(loads, (in_ref, *packed)):
        load.wait()
        one = jnp.dot(rows, ref[:width, :], preferred_element_type=F32)
        hidden.append(jax.nn.gelu(one).astype(BF16))
    loads[3].wait()
    step = 512
    for start in range(0, width, step):
        sums = jnp.dot(hidden[0], out_ref[:, start : start + step], preferred_element_type=F32)
        for one, ref in zip(hidden[1:], packed):
            count = ref.shape[1]
            blocks = [
                jnp.dot(one, ref[width + k : width + k + count, :], preferred_element_type=F32)
                for k in range(start, start + step, count)
            ]
            sums += jnp.concatenate(blocks, axis=1)
        partial_ref[:, :, start : start + step] = sums.astype(BF16).reshape(*rows_ref.shape[:2], step)


def scale_kernel(own_ref, core_ref, own_weights_ref, core_weights_ref):
    slots = own_weights_ref.shape[1]
    blocks = (own_ref, core_ref)
    stats = [ref[:, slots:].astype(F32) for ref in blocks]
    lane = lax.broadcasted_iota(jnp.int32, stats[0].shape, 1)
    highs = [jnp.sum(jnp.where(lane < 3, one, 0.0), axis=1, keepdims=True) for one in stats]
    sums = [jnp.sum(jnp.where(lane < 3, 0.0, one), axis=1, keepdims=True) for one in stats]
    top = jnp.maximum(highs[0], highs[1])
    factors = [jnp.exp(high - top) for high in highs]
    total = sums[0] * factors[0] + sums[1] * factors[1]
    for ref, out_ref, factor in zip(blocks, (own_weights_ref, core_weights_ref), factors):
        out_ref[...] = (ref[:, :slots].astype(F32) * (factor / total)).astype(BF16)


def sum_kernel(blocks_ref, before_hbm, copies_hbm, total_ref, semaphores):
    total = blocks_ref[0].astype(F32)
    for k in range(1, blocks_ref.shape[0]):
        total += blocks_ref[k].astype(F32)
    total_ref[...] = total.astype(BF16)
    copies = [started(total_ref, copies_hbm.at[k], semaphores, k) for k in range(copies_hbm.shape[0])]
    for copy in copies:
        copy.wait()


def last_kernel(near_ref, weights_ref, outs_ref, output_hbm, output_ref, semaphores):
    weights = weights_ref[...]
    step = 384
    copies = []
    for k in range(near_ref.shape[1] // step):
        part = pl.ds(k * step, step)
        far = jnp.dot(weights, outs_ref[:, part], preferred_element_type=F32)
        output_ref[:, part] = (near_ref[:, part] + far).astype(BF16)
        copies.append(started(output_ref.at[:, part], output_hbm.at[:, part], semaphores, k))
    for copy in copies:
        copy.wait()


def local(tokens, router, norm_gain, w_in, w_out):
    feats = tokens[0]
    count, width = feats.shape
    slot_count = router.shape[1]
    owners = lax.axis_size(("xhi", "z"))
    groups = lax.axis_size(("xlo", "yh"))
    per_owner = slot_count // (2 * owners)
    half = slot_count // 2
    core = lax.axis_index("core")
    hidden_units = w_in.shape[2]
    shape = jax.ShapeDtypeStruct

    partner_feats = lax.ppermute(feats, "core", other())

    ring = lax.axis_size(Y)
    most = [(2 * k + c, (k + 2 * c - 1) % ring * 2 + c) for k in range(ring) for c in range(2)]
    least = [(2 * k + c, (k + 1 - 2 * c) % ring * 2 + c) for k in range(ring) for c in range(2)]
    cut = hidden_units * 2 // 3
    given = []
    for first, units, perm in ((0, cut, most), (cut, hidden_units - cut, least)):
        packed = kernel_call(
            functools.partial(pack_kernel, first, units),
            shape((2 * width, units), BF16),
            0,
            8 * width * units,
            [HBM] * 3,
            w_in[0],
            w_out[0],
            given[0] if given else router,
            scratch=[pltpu.SemaphoreType.DMA((1 + width // units,))],
            room=16,
        )
        given.append(lax.ppermute(packed, (*Y, "core"), perm))

    copies = kernel_call(
        functools.partial(columns_kernel, per_owner),
        shape((2 * groups, router.shape[0], half), BF16),
        2 * router.shape[0] * slot_count * half,
        4 * width * half,
        [pl.BlockSpec(memory_space=pltpu.SMEM), VMEM],
        jnp.full((1,), core, jnp.int32),
        router,
        out_specs=HBM,
        scratch=[pltpu.VMEM((router.shape[0], half), BF16), pltpu.SemaphoreType.DMA((2 * groups,))],
        room=58,
    )
    columns = lax.all_to_all(copies, ("xlo", *Y), 0, 0, tiled=True).reshape(width, half)

    message = kernel_call(
        dispatch_kernel,
        shape((half, width + EXTRA), BF16),
        8 * count * width * half,
        2 * (2 * count * width + 2 * width * half),
        [HBM] * 3,
        columns,
        feats,
        partner_feats,
        out_specs=HBM,
        scratch=[
            pltpu.VMEM((width, half), BF16),
            pltpu.VMEM((count, width), BF16),
            pltpu.VMEM((count, width), BF16),
            pltpu.VMEM((half, width + EXTRA), BF16),
            pltpu.SemaphoreType.DMA((8,)),
        ],
        room=56,
    )
    received = lax.all_to_all(
        message.reshape(owners, per_owner, width + EXTRA), ("xhi", "z"), 0, 0, tiled=True
    )

    exps, answer = kernel_call(
        softmax_kernel,
        (shape((count, half + EXTRA), BF16), shape((count, half + EXTRA), BF16)),
        4 * count * width * half,
        4 * count * width,
        [VMEM] * 3,
        columns,
        feats,
        partner_feats,
        room=58,
    )
    answer = lax.ppermute(answer, "core", other())
    weights, weights_b = kernel_call(
        scale_kernel,
        (shape((count, half), BF16), shape((count, half), BF16)),
        8 * count * half,
        8 * count * half,
        [VMEM] * 2,
        exps,
        answer,
        room=16,
    )

    slots = kernel_call(
        pool_kernel,
        shape((groups, per_owner, width), BF16),
        4 * half * width,
        2 * half * width,
        [VMEM] * 2,
        received,
        norm_gain,
        out_specs=HBM,
        scratch=[pltpu.VMEM((per_owner, width), BF16), pltpu.SemaphoreType.DMA((groups,))],
        room=16,
    )
    rows = lax.all_to_all(slots, ("xlo", "yh"), 0, 0, tiled=True)
    partial = kernel_call(
        expert_kernel,
        shape((groups, per_owner, width), BF16),
        8 * groups * per_owner * width * hidden_units,
        8 * width * hidden_units,
        [VMEM, *[HBM] * 4],
        rows,
        w_in[0],
        *given,
        w_out[0],
        scratch=[
            pltpu.VMEM((width, hidden_units), BF16),
            *[pltpu.VMEM(block.shape, BF16) for block in given],
            pltpu.VMEM((hidden_units, width), BF16),
            pltpu.SemaphoreType.DMA((4,)),
        ],
        room=50,
    )
    blocks = lax.all_to_all(partial, ("xlo", "yh"), 0, 0, tiled=True)
    copies = kernel_call(
        sum_kernel,
        shape((owners, per_owner, width), BF16),
        groups * per_owner * width,
        2 * half * width,
        [VMEM, HBM],
        blocks,
        weights,
        out_specs=HBM,
        scratch=[pltpu.VMEM((per_owner, width), BF16), pltpu.SemaphoreType.DMA((owners,))],
        room=16,
    )
    outs = lax.all_to_all(copies, ("xhi", "z"), 0, 0, tiled=True).reshape(half, width)
    outs_b = lax.ppermute(outs, "core", other())

    near = feats.astype(F32) + jnp.dot(weights, outs, preferred_element_type=F32)
    return kernel_call(
        last_kernel,
        shape((count, width), BF16),
        2 * count * width * half,
        6 * count * width,
        [VMEM] * 3,
        near,
        weights_b,
        outs_b,
        out_specs=HBM,
        scratch=[pltpu.VMEM((count, width), BF16), pltpu.SemaphoreType.DMA((4,))],
        room=16,
    )[None]


def solution(mesh):
    fine = Mesh(mesh.devices.reshape(2, 4, 2, 2, 8, 2), ("xlo", "yh", "yl", "xhi", "z", "core"))
    grp, seq = ("xlo", *Y), ("xhi", "z", "core")
    in_specs = (P(grp, seq, None), P(grp, None), P(seq, None), P(seq, None, grp), P(seq, grp, None))
    return jax.shard_map(
        local, mesh=fine, in_specs=in_specs, out_specs=P(grp, seq, None), check_vma=False
    )
```

```python
import functools

import jax
import jax.numpy as jnp
from jax import lax
from jax.experimental import pallas as pl
from jax.experimental.pallas import tpu as pltpu
from jax.sharding import Mesh, PartitionSpec as P

F32 = jnp.float32
BF16 = jnp.bfloat16
EXTRA = 128
Y = ("yh", "yl")
VMEM = pl.BlockSpec(memory_space=pltpu.VMEM)
HBM = pl.BlockSpec(memory_space=pltpu.HBM)


def other(length=2):
    return [(k, k ^ 1) for k in range(length)]


def kernel_call(body, outs, flops, moved, specs, *args, out_specs=None, scratch=(), room=60):
    return pl.pallas_call(
        body,
        out_shape=outs,
        in_specs=specs,
        out_specs=jax.tree.map(lambda _: VMEM, outs) if out_specs is None else out_specs,
        scratch_shapes=scratch,
        compiler_params=pltpu.CompilerParams(vmem_limit_bytes=int(room * 2**20)),
        cost_estimate=pl.CostEstimate(flops=flops, bytes_accessed=moved, transcendentals=0),
    )(*args)


def started(source, target, semaphores, k):
    copy = pltpu.make_async_copy(source, target, semaphores.at[k])
    copy.start()
    return copy


def started_rows(source, target, semaphores, first, count):
    rows = source.shape[0] // count
    parts = [pl.ds(k * rows, rows) for k in range(count)]
    return [started(source.at[p], target.at[p], semaphores, first + k) for k, p in enumerate(parts)]


def split_off(value):
    wide = value * 65537.0
    return wide - (wide - value)


def in_lanes(columns):
    lane = lax.broadcasted_iota(jnp.int32, columns[0].shape, 1)
    packed = jnp.zeros(columns[0].shape, F32)
    for k, column in enumerate(columns):
        first = split_off(column)
        second = split_off(column - first)
        for j, piece in enumerate((first, second, column - first - second)):
            packed = jnp.where(lane == 3 * k + j, piece, packed)
    return packed.astype(BF16)


def columns_kernel(per_owner, core_ref, router_ref, copies_hbm, own_ref, semaphores):
    half = own_ref.shape[1]
    shape = (router_ref.shape[1], half)
    row = lax.broadcasted_iota(jnp.int32, shape, 0)
    col = lax.broadcasted_iota(jnp.int32, shape, 1)
    bits = per_owner.bit_length() - 1
    wanted = ((((col >> bits) << 1) + core_ref[0]) << bits) + (col & (per_owner - 1))
    pick = jnp.where(row == wanted, 1.0, 0.0).astype(BF16)
    own_ref[...] = jnp.dot(router_ref[...], pick, preferred_element_type=F32).astype(BF16)
    copies = [started(own_ref, copies_hbm.at[k], semaphores, k) for k in range(copies_hbm.shape[0])]
    for copy in copies:
        copy.wait()


def dispatch_kernel(
    columns_hbm, own_hbm, partner_hbm, message_hbm, columns_ref, own_ref, partner_ref, message_ref, semaphores
):
    width, slots = columns_ref.shape
    loads = [
        started(columns_hbm, columns_ref, semaphores, 0),
        started(own_hbm, own_ref, semaphores, 1),
        started(partner_hbm, partner_ref, semaphores, 2),
    ]
    loads[0].wait()
    columns = columns_ref[...]
    loads[1].wait()
    own_logits = jnp.dot(own_ref[...], columns, preferred_element_type=F32)
    loads[2].wait()
    partner_logits = jnp.dot(partner_ref[...], columns, preferred_element_type=F32)
    high = jnp.maximum(
        jnp.max(own_logits, axis=0, keepdims=True), jnp.max(partner_logits, axis=0, keepdims=True)
    )
    message_ref[:, width:] = in_lanes([jnp.broadcast_to(high, (EXTRA, slots)).T])
    last = pl.ds(width, EXTRA)
    stores = [started(message_ref.at[:, last], message_hbm.at[:, last], semaphores, 3)]
    own = jnp.exp(own_logits - high).astype(BF16).T
    partner = jnp.exp(partner_logits - high).astype(BF16).T
    step = 384
    for k in range(width // step):
        part = pl.ds(k * step, step)
        sums = jnp.dot(own, own_ref[:, part], preferred_element_type=F32)
        sums += jnp.dot(partner, partner_ref[:, part], preferred_element_type=F32)
        message_ref[:, part] = sums.astype(BF16)
        stores.append(started(message_ref.at[:, part], message_hbm.at[:, part], semaphores, 4 + k))
    for copy in stores:
        copy.wait()


def softmax_kernel(columns_ref, own_feats_ref, partner_feats_ref, own_ref, answer_ref):
    columns = columns_ref[...]
    for feats_ref, out_ref in ((own_feats_ref, own_ref), (partner_feats_ref, answer_ref)):
        logits = jnp.dot(feats_ref[...], columns, preferred_element_type=F32)
        slots = logits.shape[1]
        high = jnp.max(logits, axis=1, keepdims=True)
        exps = jnp.exp(logits - high)
        total = jnp.sum(exps, axis=1, keepdims=True)
        out_ref[:, :slots] = exps.astype(BF16)
        lanes = (logits.shape[0], EXTRA)
        out_ref[:, slots:] = in_lanes([jnp.broadcast_to(high, lanes), jnp.broadcast_to(total, lanes)])


def pool_kernel(received_ref, gain_ref, copies_hbm, slots_ref, semaphores):
    width = gain_ref.shape[1]
    highs = jnp.sum(received_ref[:, :, width:].astype(F32), axis=-1, keepdims=True)
    overall = jnp.max(highs, axis=0, keepdims=True)
    scale = jnp.exp(highs - overall)
    pooled = received_ref[0, :, :width].astype(F32) * scale[0]
    for k in range(1, received_ref.shape[0]):
        pooled += received_ref[k, :, :width].astype(F32) * scale[k]
    mean_sq = jnp.mean(pooled * pooled, axis=-1, keepdims=True)
    slots_ref[...] = (pooled * lax.rsqrt(mean_sq + 1e-06) * gain_ref[...]).astype(BF16)
    copies = [started(slots_ref, copies_hbm.at[k], semaphores, k) for k in range(copies_hbm.shape[0])]
    for copy in copies:
        copy.wait()


def pack_kernel(first, count, in_hbm, out_hbm, before_hbm, packed_ref, semaphores):
    width = in_hbm.shape[0]
    copies = [started(in_hbm.at[:, pl.ds(first, count)], packed_ref.at[pl.ds(0, width)], semaphores, 0)]
    for k in range(width // count):
        block = out_hbm.at[pl.ds(first, count), pl.ds(k * count, count)]
        copies.append(started(block, packed_ref.at[pl.ds(width + k * count, count)], semaphores, 1 + k))
    for copy in copies:
        copy.wait()


def expert_kernel(rows_ref, *refs):
    sources, partial_ref, targets, semaphores = refs[:4], refs[4], refs[5:9], refs[9]
    rows = rows_ref[...].reshape(-1, rows_ref.shape[-1])
    width = rows.shape[1]
    loads = [started(source, target, semaphores, k) for k, (source, target) in enumerate(zip(sources, targets))]
    in_ref, *packed, out_ref = targets
    hidden = []
    for load, ref in zip(loads, (in_ref, *packed)):
        load.wait()
        one = jnp.dot(rows, ref[:width, :], preferred_element_type=F32)
        hidden.append(jax.nn.gelu(one).astype(BF16))
    loads[3].wait()
    step = 512
    for start in range(0, width, step):
        sums = jnp.dot(hidden[0], out_ref[:, start : start + step], preferred_element_type=F32)
        for one, ref in zip(hidden[1:], packed):
            count = ref.shape[1]
            blocks = [
                jnp.dot(one, ref[width + k : width + k + count, :], preferred_element_type=F32)
                for k in range(start, start + step, count)
            ]
            sums += jnp.concatenate(blocks, axis=1)
        partial_ref[:, :, start : start + step] = sums.astype(BF16).reshape(*rows_ref.shape[:2], step)


def scale_kernel(own_ref, core_ref, own_weights_ref, core_weights_ref):
    slots = own_weights_ref.shape[1]
    blocks = (own_ref, core_ref)
    stats = [ref[:, slots:].astype(F32) for ref in blocks]
    lane = lax.broadcasted_iota(jnp.int32, stats[0].shape, 1)
    highs = [jnp.sum(jnp.where(lane < 3, one, 0.0), axis=1, keepdims=True) for one in stats]
    sums = [jnp.sum(jnp.where(lane < 3, 0.0, one), axis=1, keepdims=True) for one in stats]
    top = jnp.maximum(highs[0], highs[1])
    factors = [jnp.exp(high - top) for high in highs]
    total = sums[0] * factors[0] + sums[1] * factors[1]
    for ref, out_ref, factor in zip(blocks, (own_weights_ref, core_weights_ref), factors):
        out_ref[...] = (ref[:, :slots].astype(F32) * (factor / total)).astype(BF16)


def sum_kernel(blocks_ref, before_hbm, copies_hbm, total_ref, semaphores):
    total = blocks_ref[0].astype(F32)
    for k in range(1, blocks_ref.shape[0]):
        total += blocks_ref[k].astype(F32)
    total_ref[...] = total.astype(BF16)
    copies = [started(total_ref, copies_hbm.at[k], semaphores, k) for k in range(copies_hbm.shape[0])]
    for copy in copies:
        copy.wait()


def last_kernel(near_ref, weights_ref, outs_ref, output_hbm, output_ref, semaphores):
    weights = weights_ref[...]
    step = 384
    copies = []
    for k in range(near_ref.shape[1] // step):
        part = pl.ds(k * step, step)
        far = jnp.dot(weights, outs_ref[:, part], preferred_element_type=F32)
        output_ref[:, part] = (near_ref[:, part] + far).astype(BF16)
        copies.append(started(output_ref.at[:, part], output_hbm.at[:, part], semaphores, k))
    for copy in copies:
        copy.wait()


def local(tokens, router, norm_gain, w_in, w_out):
    feats = tokens[0]
    count, width = feats.shape
    slot_count = router.shape[1]
    owners = lax.axis_size(("xhi", "z"))
    groups = lax.axis_size(("xlo", "yh"))
    per_owner = slot_count // (2 * owners)
    half = slot_count // 2
    core = lax.axis_index("core")
    hidden_units = w_in.shape[2]
    shape = jax.ShapeDtypeStruct

    partner_feats = lax.ppermute(feats, "core", other())

    ring = lax.axis_size(Y)
    most = [(2 * k + c, (k + 2 * c - 1) % ring * 2 + c) for k in range(ring) for c in range(2)]
    least = [(2 * k + c, (k + 1 - 2 * c) % ring * 2 + c) for k in range(ring) for c in range(2)]
    cut = hidden_units * 2 // 3
    given = []
    for first, units, perm in ((0, cut, most), (cut, hidden_units - cut, least)):
        packed = kernel_call(
            functools.partial(pack_kernel, first, units),
            shape((2 * width, units), BF16),
            0,
            8 * width * units,
            [HBM] * 3,
            w_in[0],
            w_out[0],
            given[0] if given else router,
            scratch=[pltpu.SemaphoreType.DMA((1 + width // units,))],
            room=16,
        )
        given.append(lax.ppermute(packed, (*Y, "core"), perm))

    copies = kernel_call(
        functools.partial(columns_kernel, per_owner),
        shape((2 * groups, router.shape[0], half), BF16),
        2 * router.shape[0] * slot_count * half,
        4 * width * half,
        [pl.BlockSpec(memory_space=pltpu.SMEM), VMEM],
        jnp.full((1,), core, jnp.int32),
        router,
        out_specs=HBM,
        scratch=[pltpu.VMEM((router.shape[0], half), BF16), pltpu.SemaphoreType.DMA((2 * groups,))],
        room=58,
    )
    columns = lax.all_to_all(copies, ("xlo", *Y), 0, 0, tiled=True).reshape(width, half)

    message = kernel_call(
        dispatch_kernel,
        shape((half, width + EXTRA), BF16),
        8 * count * width * half,
        2 * (2 * count * width + 2 * width * half),
        [HBM] * 3,
        columns,
        feats,
        partner_feats,
        out_specs=HBM,
        scratch=[
            pltpu.VMEM((width, half), BF16),
            pltpu.VMEM((count, width), BF16),
            pltpu.VMEM((count, width), BF16),
            pltpu.VMEM((half, width + EXTRA), BF16),
            pltpu.SemaphoreType.DMA((8,)),
        ],
        room=50,
    )
    received = lax.all_to_all(
        message.reshape(owners, per_owner, width + EXTRA), ("xhi", "z"), 0, 0, tiled=True
    )

    exps, answer = kernel_call(
        softmax_kernel,
        (shape((count, half + EXTRA), BF16), shape((count, half + EXTRA), BF16)),
        4 * count * width * half,
        4 * count * width,
        [VMEM] * 3,
        columns,
        feats,
        partner_feats,
        room=58,
    )
    answer = lax.ppermute(answer, "core", other())
    weights, weights_b = kernel_call(
        scale_kernel,
        (shape((count, half), BF16), shape((count, half), BF16)),
        8 * count * half,
        8 * count * half,
        [VMEM] * 2,
        exps,
        answer,
        room=16,
    )

    slots = kernel_call(
        pool_kernel,
        shape((groups, per_owner, width), BF16),
        4 * half * width,
        2 * half * width,
        [VMEM] * 2,
        received,
        norm_gain,
        out_specs=HBM,
        scratch=[pltpu.VMEM((per_owner, width), BF16), pltpu.SemaphoreType.DMA((groups,))],
        room=16,
    )
    rows = lax.all_to_all(slots, ("xlo", "yh"), 0, 0, tiled=True)
    partial = kernel_call(
        expert_kernel,
        shape((groups, per_owner, width), BF16),
        8 * groups * per_owner * width * hidden_units,
        8 * width * hidden_units,
        [VMEM, *[HBM] * 4],
        rows,
        w_in[0],
        *given,
        w_out[0],
        scratch=[
            pltpu.VMEM((width, hidden_units), BF16),
            *[pltpu.VMEM(block.shape, BF16) for block in given],
            pltpu.VMEM((hidden_units, width), BF16),
            pltpu.SemaphoreType.DMA((4,)),
        ],
        room=50,
    )
    blocks = lax.all_to_all(partial, ("xlo", "yh"), 0, 0, tiled=True)
    copies = kernel_call(
        sum_kernel,
        shape((owners, per_owner, width), BF16),
        groups * per_owner * width,
        2 * half * width,
        [VMEM, HBM],
        blocks,
        weights,
        out_specs=HBM,
        scratch=[pltpu.VMEM((per_owner, width), BF16), pltpu.SemaphoreType.DMA((owners,))],
        room=16,
    )
    outs = lax.all_to_all(copies, ("xhi", "z"), 0, 0, tiled=True).reshape(half, width)
    outs_b = lax.ppermute(outs, "core", other())

    near = feats.astype(F32) + jnp.dot(weights, outs, preferred_element_type=F32)
    return kernel_call(
        last_kernel,
        shape((count, width), BF16),
        2 * count * width * half,
        6 * count * width,
        [VMEM] * 3,
        near,
        weights_b,
        outs_b,
        out_specs=HBM,
        scratch=[pltpu.VMEM((count, width), BF16), pltpu.SemaphoreType.DMA((4,))],
        room=16,
    )[None]


def solution(mesh):
    fine = Mesh(mesh.devices.reshape(2, 4, 2, 2, 8, 2), ("xlo", "yh", "yl", "xhi", "z", "core"))
    grp, seq = ("xlo", *Y), ("xhi", "z", "core")
    in_specs = (P(grp, seq, None), P(grp, None), P(seq, None), P(seq, None, grp), P(seq, grp, None))
    return jax.shard_map(
        local, mesh=fine, in_specs=in_specs, out_specs=P(grp, seq, None), check_vma=False
    )
```
